32 devices in a mesh: row: 8 (over z, x), col: 4 (over y, core).
Axes of the slice: x: 2, y: 2, z: 4, core: 2. Of those that a mesh axis runs over, the one named last changes fastest.
Arguments:
- left_factors: bfloat16 [32, 512, 2048], P(None, 'row', 'col'), may hold values from -0.890625 to 0.890625
- right_factors: bfloat16 [512, 131072], P('col', 'row'), may hold values from -0.890625 to 0.890625
- amplitudes: bfloat16 [512, 512, 256], P('row', 'col'), may hold values from -0.015625 to 0.015625
- eps_left: float32 [32], P('col'), may hold values from 0.2 to 1.5
- eps_right: float32 [64], replicated, may hold values from 0.2 to 1.5
- pair_energy: float32 [256], P('row'), may hold values from -2 to -0.5
Outputs:
- update: float32 [256, 32, 64], P('row', 'col')
The draws below stay inside these ranges and needn't reach their ends.
All inputs are finite; a program needn't handle non-finite values.
Results may differ from the reference program's by a relative error of at most 0.0029.
Values may be sent and summed in bfloat16 or wider, within the bound.
No kernel may reach another device: no remote copies, remote signals or barrier semaphores. Data moves between devices by JAX's collectives and lax.ppermute only.
A program may use at most 128 MiB of HBM per device.

```python
import math
import jax
import jax.numpy as jnp
from jax import lax

V = 512
NAUX = 2048
PAIRS = 256
AW = 32
BW = 64


def strengthened(array, stream_key, source, target, shards_of, factor):
    owner, partner = [(jnp.arange(array.shape[dim]) // (array.shape[dim] // shards_of)).reshape([-1 if axis == dim else 1 for axis in range(array.ndim)]) for dim in (source, target)]
    chosen = jax.random.permutation(stream_key, shards_of)[partner]
    strong = (owner == chosen) | (owner == (partner + shards_of // 2) % shards_of)
    return jnp.where(strong, factor * array, array)


def levels(key, dims, shards, least, largest):
    def one(axis_at, parts):
        steps = jax.random.uniform(jax.random.fold_in(jax.random.fold_in(key, 6), axis_at), (parts,), jnp.float32, least / len(shards), largest / len(shards))
        return jnp.repeat(jnp.exp(steps), dims[axis_at] // parts).reshape((-1,) + (1,) * (len(dims) - axis_at - 1))

    level = one(*shards[0])
    for cut in shards[1:]:
        level = level * one(*cut)
    return level


def noise(stream_key, shape, spread, limit, cuts=(), kind=jnp.bfloat16):
    level = levels(stream_key, shape, cuts, -0.22, 0.18) if cuts else 1.0
    values = jax.random.normal(stream_key, shape, jnp.float32) * spread * level
    return jnp.minimum(jnp.maximum(values, -limit), limit).astype(kind)


def noise_with(stream_key, extent, spread, reach, shards, heavy, kind=jnp.bfloat16):
    result = spread * jax.random.normal(stream_key, extent, jnp.float32)
    if shards:
        result = result * levels(stream_key, extent, shards, -0.22, 0.18)
    return jnp.clip(strengthened(result, jax.random.fold_in(stream_key, 3), *heavy), -reach, reach).astype(kind)


def setup_inputs(seed: int = 0) -> dict:
    seeds = jax.random.split(jax.random.key(seed), 7)
    return {
        "left_factors": noise(seeds[0], (AW, V, NAUX), (NAUX ** -0.25), 0.890625, ((1, 8), (2, 4))),
        "right_factors": noise(seeds[1], (V, NAUX * BW), (NAUX ** -0.25), 0.890625, ((0, 4), (1, 8))),
        "amplitudes": noise_with(seeds[2], (V, V, PAIRS), (V * V) ** -0.5, 0.015625, ((0, 8), (1, 4)), (0, 2, 8, 2.0)),
        "eps_left": jnp.clip(jnp.exp(math.log(1.5) - 2.014903 * jax.random.uniform(seeds[3], (AW,), jnp.float32) ** levels(seeds[3], (AW,), ((0, 4),), -0.2, 0.2)), 0.2, 1.5),
        "eps_right": jnp.clip(jnp.exp(jax.random.uniform(seeds[4], (BW,), jnp.float32, math.log(0.2), math.log(1.5))), 0.2, 1.5),
        "pair_energy": jnp.clip(-2.0 + 1.5 * jax.random.uniform(seeds[5], (PAIRS,), jnp.float32) ** levels(seeds[5], (PAIRS,), ((0, 8),), -0.2, 0.2), -2.0, -0.5),
    }


def reference(left_factors, right_factors, amplitudes, eps_left, eps_right, pair_energy):
    right_full = right_factors.astype(jnp.float32).reshape(V, NAUX, BW)
    amp_full = amplitudes.astype(jnp.float32)

    def one_row(left_row):
        integ = jnp.einsum("cq,dqb->cdb", left_row.astype(jnp.float32), right_full, precision=lax.Precision.HIGHEST)
        integ = lax.optimization_barrier(integ.astype(jnp.bfloat16))
        integ = integ.astype(jnp.float32)
        return jnp.einsum("cdb,cdp->pb", integ, amp_full, precision=lax.Precision.HIGHEST)

    ladder = lax.map(one_row, left_factors)
    ladder = jnp.transpose(ladder, (1, 0, 2))
    denom = eps_left[None, :, None] + eps_right[None, None, :] - pair_energy[:, None, None]
    return ladder / denom
```

```python
import functools

import jax
import jax.numpy as jnp
from jax import lax
from jax.experimental import pallas as pl
from jax.experimental.pallas import tpu as pltpu
from jax.sharding import PartitionSpec as P

AXES = ("row", "col")
CHUNKS = 4
SPLIT = 2


def contract_aux(left_piece, right_piece):
    return lax.dot_general(
        left_piece, right_piece, (((2,), (1,)), ((), ())), preferred_element_type=jnp.float32
    )


def gathered_whole(left_factors, right_factors, amplitudes, eps_left, eps_right, pair_energy):
    width_a, local_c, _ = left_factors.shape
    local_d = right_factors.shape[0]
    width_b = eps_right.shape[0]
    pairs = amplitudes.shape[2]
    gathered = lax.all_gather(right_factors, "row", axis=1, tiled=True)
    right_whole = gathered.reshape(local_d, -1, width_b)
    left_whole = lax.all_gather(left_factors, "col", axis=2, tiled=True)
    integ = contract_aux(left_whole, right_whole)
    integ = integ.astype(jnp.bfloat16)
    n_row = lax.axis_size("row")
    n_col = lax.axis_size("col")
    own_pairs = pairs // n_row
    own_a = width_a // n_col
    partial_value = jnp.einsum(
        "cdp,acdb->pab", amplitudes, integ, preferred_element_type=jnp.float32
    )
    partial_value = partial_value.reshape(pairs, width_a * width_b)
    section = lax.psum_scatter(partial_value, "row", scatter_dimension=0, tiled=True)
    ladder = lax.psum_scatter(section, "col", scatter_dimension=1, tiled=True)
    ladder = ladder.reshape(own_pairs, own_a, width_b)
    denom = eps_left[None, :, None] + eps_right[None, None, :] - pair_energy[:, None, None]
    return ladder / denom


def ladder_kernel(slots, which_ref, *refs):
    pieces = refs[:slots]
    left_ref, amp_own_ref, amp_other_ref, add_ref, out_ref = refs[slots:]
    depth, width_b, width_q = pieces[0].shape
    tile_a, _, chunk_c, _ = left_ref.shape[2:]
    span = 2 * chunk_c
    integ = None
    for s in range(slots):
        left = left_ref[which_ref[2 * s], which_ref[2 * s + 1]].reshape(tile_a * span, width_q)
        right = pieces[s][...].reshape(depth * width_b, width_q)
        term = lax.dot_general(
            right, left, (((1,), (1,)), ((), ())), preferred_element_type=jnp.float32
        )
        integ = term if integ is None else integ + term
    integ = integ.astype(jnp.bfloat16)
    integ = jnp.concatenate(
        [
            jnp.concatenate(
                [
                    integ[d * width_b : (d + 1) * width_b, a * span : (a + 1) * span]
                    for d in range(depth)
                ],
                axis=1,
            )
            for a in range(tile_a)
        ],
        axis=0,
    )
    amp = jnp.concatenate([amp_own_ref[...], amp_other_ref[...]], axis=1)
    amp = amp.reshape(depth * span, -1)
    out = jnp.dot(integ, amp, preferred_element_type=jnp.float32)
    out_ref[...] = add_ref[...] + out.reshape(out_ref.shape)


def add_ladder(pieces, which, left, amp_own, amp_other, add, tile_a=4):
    slots = len(pieces)
    depth, width_b, width_q = pieces[0].shape
    width_a, _, chunk_c, _ = left.shape[2:]
    pairs = amp_own.shape[-1]

    def whole(array):
        return pl.BlockSpec(array.shape, lambda i, w: (0,) * array.ndim)

    left_spec = pl.BlockSpec(
        left.shape[:2] + (tile_a,) + left.shape[3:], lambda i, w: (0, 0, i, 0, 0, 0)
    )
    out_spec = pl.BlockSpec((tile_a, width_b, pairs), lambda i, w: (i, 0, 0))
    products = depth * width_b * width_a * 2 * chunk_c * (slots * width_q + pairs)
    moved = sum(2 * v.size for v in (*pieces, left, amp_own, amp_other)) + 8 * add.size
    return pl.pallas_call(
        functools.partial(ladder_kernel, slots),
        grid_spec=pltpu.PrefetchScalarGridSpec(
            num_scalar_prefetch=1,
            grid=(width_a // tile_a,),
            in_specs=[whole(v) for v in pieces]
            + [left_spec, whole(amp_own), whole(amp_other), out_spec],
            out_specs=out_spec,
        ),
        out_shape=jax.ShapeDtypeStruct(add.shape, jnp.float32),
        input_output_aliases={slots + 4: 0},
        cost_estimate=pl.CostEstimate(flops=2 * products, bytes_accessed=moved, transcendentals=0),
        compiler_params=pltpu.CompilerParams(vmem_limit_bytes=52 * 2**20),
        name="ladder",
    )(which, *pieces, left, amp_own, amp_other, add)


def by_lines(n_row, n_col, *arrays):
    left_factors, right_factors, amplitudes, eps_left, eps_right, pair_energy = arrays
    row, col = lax.axis_index("row"), lax.axis_index("col")
    n_z, n_y = n_row // 2, n_col // 2
    z, x, y, core = row // 2, row % 2, col // 2, col % 2
    half = n_z // 2

    def inner(at):
        return at in (half - 1, half)

    def send(value, place):
        pairs = []
        for at_z in range(n_z):
            for at_x in range(2):
                for at_y in range(n_y):
                    for at_k in range(2):
                        to = place(at_z, at_x, at_y, at_k)
                        if to is not None:
                            source = (at_z * 2 + at_x) * n_col + at_y * 2 + at_k
                            target = (to[0] * 2 + to[1]) * n_col + to[2] * 2 + to[3]
                            pairs.append((source, target))
        return lax.ppermute(value, AXES, pairs)

    def other_x(c, x, y, k):
        return c, 1 - x, y, k

    def other_y(c, x, y, k):
        return c, x, 1 - y, k

    def other_core(c, x, y, k):
        return c, x, y, 1 - k

    def near(c, x, y, k):
        return c ^ 1, x, y, k

    def across(c, x, y, k):
        return (n_z - 1 - c, x, y, k) if inner(c) else None

    def outward(c, x, y, k):
        return (c ^ 1, x, y, k) if inner(c) else None

    def inward(c, x, y, k):
        return None if inner(c) else (c ^ 1, x, y, k)

    def far_y(c):
        return 1 - c // half

    is_inner = (z == half - 1) | (z == half)

    def pick(value, at):
        return lax.dynamic_index_in_dim(value, at, 0, keepdims=False)

    local_d = right_factors.shape[0]
    width_b = eps_right.shape[0]
    depth = local_d // 2 // CHUNKS
    right = right_factors.reshape(2, CHUNKS, depth, -1, width_b)
    chunks = range(CHUNKS)
    right_keep, right_give = pick(right, x), pick(right, 1 - x)
    give = [right_give[i].transpose(0, 2, 1) for i in chunks]
    own = [right_keep[i].transpose(0, 2, 1) for i in chunks]
    far = [send(v, other_x) for v in give]
    blocks = []
    for i in chunks:
        zero = (own[i], far[i])
        one = tuple(send(v, near) for v in zero)
        two = tuple(send(v, across) for v in zero)
        three = tuple(send(v, across) for v in one)
        if i < CHUNKS - SPLIT:
            two, three = (
                tuple(jnp.where(is_inner, v, send(v, outward)) for v in pair)
                for pair in (two, three)
            )
        blocks.append((*zero, *one, *two, *three))

    local_c, _, pairs = amplitudes.shape
    amp = amplitudes.reshape(local_c, 2, CHUNKS, depth, pairs)
    amp_keep = lax.dynamic_index_in_dim(amp, x, 1, keepdims=False)
    amp_give = lax.dynamic_index_in_dim(amp, 1 - x, 1, keepdims=False)
    amp_own = [amp_keep[:, i].transpose(1, 0, 2) for i in chunks]
    amp_far = [send(amp_give[:, i].transpose(1, 0, 2), other_x) for i in chunks]

    width_a, _, local_q = left_factors.shape
    mine = left_factors.reshape(width_a, local_c, 2, local_q // 2).transpose(2, 0, 1, 3)
    mine_x = send(mine, other_x)
    here = jnp.stack([mine, mine_x], axis=2)
    here_y = jnp.stack([send(mine, other_y), send(mine_x, other_y)], axis=2)
    left = jnp.stack([here, send(here, other_core), here_y, send(here_y, other_core)])

    def in_far(c, x, y, k):
        return (c ^ 1, x, y, k) if not inner(c) and y == far_y(c) else None

    def far_x(c, x, y, k):
        return (c, 1 - x, y, k) if inner(c) and y == far_y(c) else None

    def far_to_y(c, x, y, k):
        return (c, x, 1 - y, k) if inner(c) and y == far_y(c) else None

    got = send(mine, in_far)
    got_x = send(got, far_x)
    got, got_x = (jnp.where(y == far_y(z), v, send(v, far_to_y)) for v in (got, got_x))
    end = jnp.stack([got, got_x], axis=2)
    end = jnp.stack([end, send(end, other_core)])

    far_inner = jnp.where(z < half, half, half - 1)
    planes = (z, z ^ 1, far_inner, far_inner ^ 1)
    which = jnp.stack([v for p in planes for v in (p ^ col, x, p ^ col, 1 - x)])
    which_end = jnp.stack([v for p in planes[2:] for v in ((p % 2) ^ core, x, (p % 2) ^ core, 1 - x)])
    total = jnp.zeros((width_a, width_b, pairs), jnp.float32)
    for i in chunks:
        total = add_ladder(blocks[i], which, left, amp_own[i], amp_far[i], total)
        if i >= CHUNKS - SPLIT:
            amp_end = [send(v, inward) for v in (amp_own[i], amp_far[i])]
            total = add_ladder(blocks[i][4:], which_end, end, *amp_end, total)

    own_a, own_pairs = width_a // n_col, pairs // n_row
    total = total.reshape(n_y, 2, own_a, width_b, pairs)
    keep = lax.dynamic_index_in_dim(total, core, 1, keepdims=False)
    give = lax.dynamic_index_in_dim(total, 1 - core, 1, keepdims=False)
    part = keep + send(give, other_core)
    part = part.reshape(n_y, own_a * width_b, n_z, 2, own_pairs).transpose(3, 0, 2, 4, 1)

    def over_x(v):
        return pick(v, x) + send(pick(v, 1 - x), other_x)

    def over_y(v):
        return pick(v, y) + send(pick(v, 1 - y), other_y)

    cut = own_pairs // 2
    first = over_y(over_x(part[:, :, :, :cut]))
    second = over_x(over_y(part[:, :, :, cut:].transpose(1, 0, 2, 3, 4)))
    part = jnp.concatenate([first, second], axis=1)
    ladder = pick(part, z)
    for step in range(1, n_z):
        ladder = ladder + send(pick(part, z ^ step), lambda c, x, y, k, s=step: (c ^ s, x, y, k))
    ladder = ladder.reshape(own_pairs, own_a, width_b)
    denom = eps_left[None, :, None] + eps_right[None, None, :] - pair_energy[:, None, None]
    return ladder / denom


def solution(mesh):
    n_row, n_col = mesh.shape["row"], mesh.shape["col"]
    lines = n_row == 2 * n_col and n_col == 4
    per_device = functools.partial(by_lines, n_row, n_col) if lines else gathered_whole
    in_specs = (
        P(None, "row", "col"),
        P("col", "row"),
        P("row", "col", None),
        P("col"),
        P(),
        P("row"),
    )
    out_specs = P("row", "col", None)
    return jax.shard_map(
        per_device, mesh=mesh, in_specs=in_specs, out_specs=out_specs, check_vma=False
    )
```

```python
import functools

import jax
import jax.numpy as jnp
from jax import lax
from jax.experimental import pallas as pl
from jax.experimental.pallas import tpu as pltpu
from jax.sharding import PartitionSpec as P

AXES = ("row", "col")
IN_FLIGHT = 5


def contract_aux(left_piece, right_piece):
    return lax.dot_general(
        left_piece, right_piece, (((2,), (1,)), ((), ())), preferred_element_type=jnp.float32
    )


def gathered_whole(left_factors, right_factors, amplitudes, eps_left, eps_right, pair_energy):
    width_a, local_c, _ = left_factors.shape
    local_d = right_factors.shape[0]
    width_b = eps_right.shape[0]
    pairs = amplitudes.shape[2]
    gathered = lax.all_gather(right_factors, "row", axis=1, tiled=True)
    right_whole = gathered.reshape(local_d, -1, width_b)
    left_whole = lax.all_gather(left_factors, "col", axis=2, tiled=True)
    integ = contract_aux(left_whole, right_whole)
    integ = integ.astype(jnp.bfloat16)
    n_row = lax.axis_size("row")
    n_col = lax.axis_size("col")
    own_pairs = pairs // n_row
    own_a = width_a // n_col
    partial_value = jnp.einsum(
        "cdp,acdb->pab", amplitudes, integ, preferred_element_type=jnp.float32
    )
    partial_value = partial_value.reshape(pairs, width_a * width_b)
    section = lax.psum_scatter(partial_value, "row", scatter_dimension=0, tiled=True)
    ladder = lax.psum_scatter(section, "col", scatter_dimension=1, tiled=True)
    ladder = ladder.reshape(own_pairs, own_a, width_b)
    denom = eps_left[None, :, None] + eps_right[None, None, :] - pair_energy[:, None, None]
    return ladder / denom


def ladder_kernel(slots, n_left, first, which_ref, *refs):
    pieces, refs = refs[:slots], refs[slots:]
    lefts, refs = refs[: 4 * n_left], refs[4 * n_left :]
    amp_own_ref, amp_other_ref, *add_ref, out_ref, held, sems = refs
    depth, width_b, width_q = pieces[0].shape
    _, _, _, tile_a, _, chunk_c, _ = held.shape
    span = 2 * chunk_c
    step, steps = pl.program_id(0), pl.num_programs(0)

    def copies(at, slot):
        rows = pl.ds(pl.multiple_of(at * tile_a, tile_a), tile_a)
        return [
            pltpu.make_async_copy(
                lefts[4 * r + 2 * s + h].at[rows], held.at[slot, r, h, :, s], sems.at[slot, r, s, h]
            )
            for r in range(n_left)
            for s in range(2)
            for h in range(2)
        ]

    @pl.when(step == 0)
    def _():
        for copy in copies(step, 0):
            copy.start()

    slot = lax.rem(step, 2)

    @pl.when(step + 1 < steps)
    def _():
        for copy in copies(step + 1, 1 - slot):
            copy.start()

    for copy in copies(step, slot):
        copy.wait()

    integ = None
    for s in range(slots):
        left = held[slot, which_ref[2 * s], which_ref[2 * s + 1]].reshape(tile_a * span, width_q)
        right = pieces[s][...].reshape(depth * width_b, width_q)
        term = lax.dot_general(
            right, left, (((1,), (1,)), ((), ())), preferred_element_type=jnp.float32
        )
        integ = term if integ is None else integ + term
    integ = integ.astype(jnp.bfloat16)
    integ = jnp.concatenate(
        [
            jnp.concatenate(
                [
                    integ[d * width_b : (d + 1) * width_b, a * span : (a + 1) * span]
                    for d in range(depth)
                ],
                axis=1,
            )
            for a in range(tile_a)
        ],
        axis=0,
    )
    amp = jnp.concatenate([amp_own_ref[...], amp_other_ref[...]], axis=1)
    amp = amp.reshape(depth * span, -1)
    out = jnp.dot(integ, amp, preferred_element_type=jnp.float32).reshape(out_ref.shape)
    out_ref[...] = out if first else add_ref[0][...] + out


def add_ladder(pieces, which, lefts, amps, add, depth, tile_a=4):
    slots, n_left = len(pieces), len(lefts) // 4
    width_b, width_q = pieces[0][0].shape[-2:]
    width_a, chunk_c = lefts[0].shape[:2]
    pairs = amps[0][0].shape[-1]

    def chunk_of(array, at):
        if array.ndim == 4:
            return pl.BlockSpec((None, *array.shape[1:]), lambda i, w: (at, 0, 0, 0))
        return pl.BlockSpec((depth, *array.shape[1:]), lambda i, w: (at, 0, 0))

    out_spec = pl.BlockSpec((tile_a, width_b, pairs), lambda i, w: (i, 0, 0))
    products = depth * width_b * width_a * 2 * chunk_c * (slots * width_q + pairs)
    moved = 2 * depth * (slots * width_b * width_q + 2 * chunk_c * pairs)
    moved += sum(2 * v.size for v in lefts) + 8 * width_a * width_b * pairs
    more = () if add is None else (add,)
    return pl.pallas_call(
        functools.partial(ladder_kernel, slots, n_left, add is None),
        grid_spec=pltpu.PrefetchScalarGridSpec(
            num_scalar_prefetch=1,
            grid=(width_a // tile_a,),
            in_specs=[chunk_of(*v) for v in pieces]
            + [pl.BlockSpec(memory_space=pl.ANY)] * len(lefts)
            + [chunk_of(*v) for v in amps]
            + [out_spec] * len(more),
            out_specs=out_spec,
            scratch_shapes=[
                pltpu.VMEM((2, n_left, 2, tile_a, 2, chunk_c, width_q), jnp.bfloat16),
                pltpu.SemaphoreType.DMA((2, n_left, 2, 2)),
            ],
        ),
        out_shape=jax.ShapeDtypeStruct((width_a, width_b, pairs), jnp.float32),
        input_output_aliases={slots + len(lefts) + 3: 0} if more else {},
        cost_estimate=pl.CostEstimate(flops=2 * products, bytes_accessed=moved, transcendentals=0),
        compiler_params=pltpu.CompilerParams(vmem_limit_bytes=32 * 2**20),
        name="ladder",
    )(which, *(v for v, _ in pieces), *lefts, *(v for v, _ in amps), *more)


def by_lines(n_row, n_col, *arrays):
    left_factors, right_factors, amplitudes, eps_left, eps_right, pair_energy = arrays
    row, col = lax.axis_index("row"), lax.axis_index("col")
    n_z, n_y = n_row // 2, n_col // 2
    z, x, y, core = row // 2, row % 2, col // 2, col % 2
    half = n_z // 2

    def inner(at):
        return at in (half - 1, half)

    issued = []
    latest = []

    def send(value, place):
        pairs = []
        for at_z in range(n_z):
            for at_x in range(2):
                for at_y in range(n_y):
                    for at_k in range(2):
                        to = place(at_z, at_x, at_y, at_k)
                        if to is not None:
                            source = (at_z * 2 + at_x) * n_col + at_y * 2 + at_k
                            target = (to[0] * 2 + to[1]) * n_col + to[2] * 2 + to[3]
                            pairs.append((source, target))
        value, *_ = lax.optimization_barrier((value, *issued[-IN_FLIGHT:][:1], *latest))
        got = lax.ppermute(value, AXES, pairs)
        issued.append(got)
        return got

    def other_x(c, x, y, k):
        return c, 1 - x, y, k

    def other_y(c, x, y, k):
        return c, x, 1 - y, k

    def other_core(c, x, y, k):
        return c, x, y, 1 - k

    def near(c, x, y, k):
        return c ^ 1, x, y, k

    def across(c, x, y, k):
        return (n_z - 1 - c, x, y, k) if inner(c) else None

    def outward(c, x, y, k):
        return (c ^ 1, x, y, k) if inner(c) else None

    def between_inner(step):
        return lambda c, x, y, k: step(c, x, y, k) if inner(c) else None

    is_inner = (z == half - 1) | (z == half)
    at_far = y == 1 - z // half

    width_a, local_c, local_q = left_factors.shape
    mine = left_factors.reshape(width_a, local_c, 2, local_q // 2).transpose(2, 0, 1, 3)

    local_d = right_factors.shape[0]
    width_b = eps_right.shape[0]
    part_d = local_d // 4
    depth = part_d // 2

    def right_part(at_x, part):
        rows = lax.dynamic_slice_in_dim(right_factors, at_x * 2 * part_d + part * part_d, part_d)
        return rows.reshape(part_d, -1, width_b).transpose(0, 2, 1)

    def amp_part(at_x, part):
        got = lax.dynamic_slice_in_dim(amplitudes, at_x * 2 * part_d + part * part_d, part_d, 1)
        return got.transpose(1, 0, 2)

    def both(one, two, at):
        rows = slice(at * depth, (at + 1) * depth)
        return jnp.stack([one[rows], two[rows]])

    def swap(inner_one, end_one):
        return send(jnp.where(is_inner, inner_one, end_one.reshape(inner_one.shape)), near)

    far_inner = jnp.where(z < half, half, half - 1)
    planes = (z, z ^ 1, far_inner, far_inner ^ 1)
    which = jnp.stack([v for p in planes for v in (p ^ col, x, p ^ col, 1 - x)])
    turn = at_far.astype(x.dtype)
    which_end = jnp.stack(
        [v for p in planes[2:] for v in ((p % 2) ^ core, x ^ turn, (p % 2) ^ core, 1 - x ^ turn)]
    )

    y_0 = send(mine[0], other_y)
    x_full = send(right_part(1 - x, 0), other_x)
    o_full = right_part(x, 0)
    near_o = send(o_full, near)
    far_o = send(o_full, across)
    mine_k = send(mine, other_core)
    y_1 = send(mine[1], other_y)
    x_0 = send(mine[0], other_x)
    near_x = send(x_full, near)
    far_x = send(x_full, across)
    yk_0 = send(y_0, other_core)
    x_1 = send(mine[1], other_x)
    xy_0 = send(x_0, other_y)
    third_o = send(near_o, across)
    far_full = [both(far_o, far_x, i) for i in range(2)]
    e3 = swap(far_full[0], jnp.where(at_far, mine[1], y_0))
    yk_1 = send(y_1, other_core)
    x_split = send(right_part(1 - x, 1), other_x)
    xy_1 = send(x_1, other_y)
    e4 = send(far_full[1], outward)
    third_x = send(near_x, across)
    xk_0 = send(x_0, other_core)
    amp_full = (amp_part(x, 0), send(amp_part(1 - x, 0), other_x))
    xk_1 = send(x_1, other_core)
    o_split = right_part(x, 1)
    split = [both(o_split, x_split, i) for i in range(2)]
    third_full = [both(third_o, third_x, i) for i in range(2)]
    far_split, third_split = [None, None], [None, None]
    e5 = swap(third_full[0], split[0])
    far_split[0] = send(split[0], across)
    xyk_0 = send(xy_0, other_core)
    xyk_1 = send(xy_1, other_core)
    e6 = swap(third_full[1], split[1])
    amp_split = (amp_part(x, 1), send(amp_part(1 - x, 1), other_x))
    third_split[0] = send(e5, across)
    lefts = (mine[0], mine[1], x_0, x_1, mine_k[0], mine_k[1], xk_0, xk_1)
    lefts += (y_0, y_1, xy_0, xy_1, yk_0, yk_1, xyk_0, xyk_1)

    def full(i, out_far, out_third, total):
        far = jnp.where(is_inner, far_full[i], out_far)
        third = jnp.where(is_inner, third_full[i], out_third)
        pieces = [(o_full, i), (x_full, i), (near_o, i), (near_x, i)]
        pieces += [(far, 0), (far, 1), (third, 0), (third, 1)]
        return add_ladder(pieces, which, lefts, [(v, i) for v in amp_full], total, depth)

    def parted(i, e_in, e_out, total):
        beside = jnp.where(is_inner, e_in, e_out)
        pieces = [(v, h) for v in (split[i], beside, far_split[i], third_split[i]) for h in range(2)]
        return add_ladder(pieces, which, lefts, [(v, i) for v in amp_split], total, depth)

    def ended(i, amp_end, total):
        pieces = [(v, h) for v in (far_split[i], third_split[i]) for h in range(2)]
        return add_ladder(pieces, which_end, ends, [(amp_end, 0), (amp_end, 1)], total, depth)

    total = full(0, e3, e5, None)
    latest[:] = [total]
    far_split[1] = send(split[1], across)
    amp_both = [both(*amp_split, i) for i in range(2)]
    e7 = swap(split[0], amp_both[0])
    end_own = e3.reshape(y_0.shape)
    end_y = send(end_own, between_inner(other_y))
    end_x = send(end_own, between_inner(other_x))
    total = full(1, e4, e6, total)
    latest[:] = [total]
    third_split[1] = send(e6, across)
    e8 = swap(split[1], amp_both[1])
    end_xy = send(end_x, between_inner(other_y))
    ends = (end_own, end_y, end_x, end_xy)
    total = parted(0, e5, e7, total)
    latest[:] = [total]
    ends += tuple(send(v, other_core) for v in ends)
    total = parted(1, e6, e8, total)
    total = ended(0, e7, total)
    total = ended(1, e8, total)
    latest[:] = []
    issued[:] = []

    def pick(value, at):
        return lax.dynamic_index_in_dim(value, at, 0, keepdims=False)

    pairs = amplitudes.shape[2]
    own_a, own_pairs = width_a // n_col, pairs // n_row
    total = total.reshape(n_y, 2, own_a, width_b, pairs)
    keep = lax.dynamic_index_in_dim(total, core, 1, keepdims=False)
    give = lax.dynamic_index_in_dim(total, 1 - core, 1, keepdims=False)
    part = keep + send(give, other_core)
    part = part.reshape(n_y, own_a * width_b, n_z, 2, own_pairs).transpose(3, 0, 2, 4, 1)

    def over_x(v):
        return pick(v, x) + send(pick(v, 1 - x), other_x)

    def over_y(v):
        return pick(v, y) + send(pick(v, 1 - y), other_y)

    cut = own_pairs // 2
    first = over_y(over_x(part[:, :, :, :cut]))
    second = over_x(over_y(part[:, :, :, cut:].transpose(1, 0, 2, 3, 4)))
    part = jnp.concatenate([first, second], axis=1)
    ladder = pick(part, z)
    for step in range(1, n_z):
        ladder = ladder + send(pick(part, z ^ step), lambda c, x, y, k, s=step: (c ^ s, x, y, k))
    ladder = ladder.reshape(own_pairs, own_a, width_b)
    denom = eps_left[None, :, None] + eps_right[None, None, :] - pair_energy[:, None, None]
    return ladder / denom


def solution(mesh):
    n_row, n_col = mesh.shape["row"], mesh.shape["col"]
    lines = n_row == 2 * n_col and n_col == 4
    per_device = functools.partial(by_lines, n_row, n_col) if lines else gathered_whole
    in_specs = (
        P(None, "row", "col"),
        P("col", "row"),
        P("row", "col", None),
        P("col"),
        P(),
        P("row"),
    )
    out_specs = P("row", "col", None)
    return jax.shard_map(
        per_device, mesh=mesh, in_specs=in_specs, out_specs=out_specs, check_vma=False
    )
```

```python
import functools

import jax
import jax.numpy as jnp
from jax import lax
from jax.experimental import pallas as pl
from jax.experimental.pallas import tpu as pltpu
from jax.sharding import PartitionSpec as P

AXES = ("row", "col")


def contract_aux(left_piece, right_piece):
    return lax.dot_general(
        left_piece, right_piece, (((2,), (1,)), ((), ())), preferred_element_type=jnp.float32
    )


def gathered_whole(left_factors, right_factors, amplitudes, eps_left, eps_right, pair_energy):
    width_a, local_c, _ = left_factors.shape
    local_d = right_factors.shape[0]
    width_b = eps_right.shape[0]
    pairs = amplitudes.shape[2]
    gathered = lax.all_gather(right_factors, "row", axis=1, tiled=True)
    right_whole = gathered.reshape(local_d, -1, width_b)
    left_whole = lax.all_gather(left_factors, "col", axis=2, tiled=True)
    integ = contract_aux(left_whole, right_whole)
    integ = integ.astype(jnp.bfloat16)
    n_row = lax.axis_size("row")
    n_col = lax.axis_size("col")
    own_pairs = pairs // n_row
    own_a = width_a // n_col
    partial_value = jnp.einsum(
        "cdp,acdb->pab", amplitudes, integ, preferred_element_type=jnp.float32
    )
    partial_value = partial_value.reshape(pairs, width_a * width_b)
    section = lax.psum_scatter(partial_value, "row", scatter_dimension=0, tiled=True)
    ladder = lax.psum_scatter(section, "col", scatter_dimension=1, tiled=True)
    ladder = ladder.reshape(own_pairs, own_a, width_b)
    denom = eps_left[None, :, None] + eps_right[None, None, :] - pair_energy[:, None, None]
    return ladder / denom


def ladder_kernel(slots, n_left, choices, places, first, which_ref, *refs):
    pieces, refs = refs[:slots], refs[slots:]
    lefts, refs = refs[: 4 * n_left * choices], refs[4 * n_left * choices :]
    amp_own_ref, amp_other_ref, *add_ref, out_ref, held, sems = refs
    depth, width_b, width_q = pieces[0].shape
    _, _, _, tile_a, _, chunk_c, _ = held.shape
    span = 2 * chunk_c
    step, steps = pl.program_id(0), pl.num_programs(0)

    def copies(at, slot, choice=0):
        rows = pl.ds(pl.multiple_of(at * tile_a, tile_a), tile_a)

        def source(n):
            return lefts[n].at[rows] if places[n] is None else lefts[n].at[places[n], rows]

        return [
            pltpu.make_async_copy(
                source(4 * (choice * n_left + r) + 2 * s + h),
                held.at[slot, r, h, :, s],
                sems.at[slot, r, s, h],
            )
            for r in range(n_left)
            for s in range(2)
            for h in range(2)
        ]

    def start(at, slot):
        for choice in range(choices):

            @pl.when(which_ref[2 * slots] == choice)
            def _():
                for copy in copies(at, slot, choice):
                    copy.start()

    slot = lax.rem(step, 2)

    @pl.when(step == 0)
    def _():
        start(step, 0)

    @pl.when(step + 1 < steps)
    def _():
        start(step + 1, 1 - slot)

    for copy in copies(step, slot):
        copy.wait()

    integ = None
    for s in range(slots):
        left = held[slot, which_ref[2 * s], which_ref[2 * s + 1]].reshape(tile_a * span, width_q)
        right = pieces[s][...].reshape(depth * width_b, width_q)
        term = lax.dot_general(
            right, left, (((1,), (1,)), ((), ())), preferred_element_type=jnp.float32
        )
        integ = term if integ is None else integ + term
    integ = integ.astype(jnp.bfloat16)
    integ = jnp.concatenate(
        [
            jnp.concatenate(
                [
                    integ[d * width_b : (d + 1) * width_b, a * span : (a + 1) * span]
                    for d in range(depth)
                ],
                axis=1,
            )
            for a in range(tile_a)
        ],
        axis=0,
    )
    amp = jnp.concatenate([amp_own_ref[...], amp_other_ref[...]], axis=1)
    amp = amp.reshape(depth * span, -1)
    out = jnp.dot(integ, amp, preferred_element_type=jnp.float32).reshape(out_ref.shape)
    out_ref[...] = out if first else add_ref[0][...] + out


def add_ladder(pieces, which, lefts, amps, add, depth, choices=1, tile_a=4):
    slots, n_left = len(pieces), len(lefts) // 4 // choices
    places = [v[1] if isinstance(v, tuple) else None for v in lefts]
    lefts = [v[0] if isinstance(v, tuple) else v for v in lefts]
    width_b, width_q = pieces[0][0].shape[-2:]
    width_a, chunk_c = lefts[0].shape[-3:-1]
    pairs = amps[0][0].shape[-1]

    def chunk_of(array, at):
        if array.ndim == 4:
            return pl.BlockSpec((None, *array.shape[1:]), lambda i, w: (at, 0, 0, 0))
        return pl.BlockSpec((depth, *array.shape[1:]), lambda i, w: (at, 0, 0))

    out_spec = pl.BlockSpec((tile_a, width_b, pairs), lambda i, w: (i, 0, 0))
    products = depth * width_b * width_a * 2 * chunk_c * (slots * width_q + pairs)
    moved = 2 * depth * (slots * width_b * width_q + 2 * chunk_c * pairs)
    moved += 8 * n_left * width_a * chunk_c * width_q + 8 * width_a * width_b * pairs
    more = () if add is None else (add,)
    return pl.pallas_call(
        functools.partial(ladder_kernel, slots, n_left, choices, places, add is None),
        grid_spec=pltpu.PrefetchScalarGridSpec(
            num_scalar_prefetch=1,
            grid=(width_a // tile_a,),
            in_specs=[chunk_of(*v) for v in pieces]
            + [pl.BlockSpec(memory_space=pl.ANY)] * len(lefts)
            + [chunk_of(*v) for v in amps]
            + [out_spec] * len(more),
            out_specs=out_spec,
            scratch_shapes=[
                pltpu.VMEM((2, n_left, 2, tile_a, 2, chunk_c, width_q), jnp.bfloat16),
                pltpu.SemaphoreType.DMA((2, n_left, 2, 2)),
            ],
        ),
        out_shape=jax.ShapeDtypeStruct((width_a, width_b, pairs), jnp.float32),
        input_output_aliases={slots + len(lefts) + 3: 0} if more else {},
        cost_estimate=pl.CostEstimate(flops=2 * products, bytes_accessed=moved, transcendentals=0),
        compiler_params=pltpu.CompilerParams(vmem_limit_bytes=32 * 2**20),
        name="ladder",
    )(which, *(v for v, _ in pieces), *lefts, *(v for v, _ in amps), *more)


def by_lines(n_row, n_col, *arrays):
    left_factors, right_factors, amplitudes, eps_left, eps_right, pair_energy = arrays
    row, col = lax.axis_index("row"), lax.axis_index("col")
    n_z, n_y = n_row // 2, n_col // 2
    z, x, y, core = row // 2, row % 2, col // 2, col % 2
    half = n_z // 2

    def inner(at):
        return at in (half - 1, half)

    before = []

    def send(value, place):
        pairs = []
        for at_z in range(n_z):
            for at_x in range(2):
                for at_y in range(n_y):
                    for at_k in range(2):
                        to = place(at_z, at_x, at_y, at_k)
                        if to is not None:
                            source = (at_z * 2 + at_x) * n_col + at_y * 2 + at_k
                            target = (to[0] * 2 + to[1]) * n_col + to[2] * 2 + to[3]
                            pairs.append((source, target))
        return lax.ppermute(value, AXES, pairs)

    def now(*values):
        return lax.optimization_barrier((values, tuple(before)))[0]

    def step(*transfers, beside=()):
        values = now(*(value for value, _ in transfers))
        got = [send(value, place) for value, (_, place) in zip(values, transfers)]
        before[:] = [*got, *beside]
        return got

    def other_x(c, x, y, k):
        return c, 1 - x, y, k

    def other_y(c, x, y, k):
        return c, x, 1 - y, k

    def other_core(c, x, y, k):
        return c, x, y, 1 - k

    def near(c, x, y, k):
        return c ^ 1, x, y, k

    def across(c, x, y, k):
        return (n_z - 1 - c, x, y, k) if inner(c) else None

    def outward(c, x, y, k):
        return (c ^ 1, x, y, k) if inner(c) else None

    def between_inner(step):
        return lambda c, x, y, k: step(c, x, y, k) if inner(c) else None

    is_inner = (z == half - 1) | (z == half)
    at_far = y == 1 - z // half

    width_a, local_c, local_q = left_factors.shape
    mine = left_factors.reshape(width_a, local_c, 2, local_q // 2).transpose(2, 0, 1, 3)

    local_d = right_factors.shape[0]
    width_b = eps_right.shape[0]
    part_d = local_d // 4
    depth = part_d // 2

    def right_part(at_x, part, right=right_factors):
        rows = lax.dynamic_slice_in_dim(right, at_x * 2 * part_d + part * part_d, part_d)
        return rows.reshape(part_d, -1, width_b).transpose(0, 2, 1)

    def amp_part(at_x, part, amp):
        got = lax.dynamic_slice_in_dim(amp, at_x * 2 * part_d + part * part_d, part_d, 1)
        return got.transpose(1, 0, 2)

    def both(one, two, at):
        rows = slice(at * depth, (at + 1) * depth)
        return jnp.stack([one[rows], two[rows]])

    def either(inner_one, end_one):
        return jnp.where(is_inner, inner_one, end_one.reshape(inner_one.shape)), near

    far_inner = jnp.where(z < half, half, half - 1)
    planes = (z, z ^ 1, far_inner, far_inner ^ 1)
    which = jnp.stack([v for p in planes for v in (p ^ col, x, p ^ col, 1 - x)] + [jnp.zeros_like(x)])
    turn = jnp.where(is_inner & at_far, 1, 0)
    choice = jnp.where(is_inner, 0, jnp.where(at_far, 1, 2))
    which_far = [v for p in planes[2:] for v in ((p % 2) ^ core, x ^ turn, (p % 2) ^ core, 1 - x ^ turn)]
    which_far = jnp.stack(which_far + [choice])

    mine, x_give, o_full = lax.optimization_barrier((mine, right_part(1 - x, 0), right_part(x, 0)))
    before[:] = [x_give, o_full]
    (right_later,) = now(right_factors)
    near_o, far_o, x_full, y_0 = step(
        (o_full, near), (o_full, across), (x_give, other_x), (mine[0], other_y)
    )
    give_split, o_split = right_part(1 - x, 1, right_later), right_part(x, 1, right_later)
    before += [give_split, o_split]

    (amp_later,) = now(amplitudes)
    out_o, far_x, x_0, y_1, mine_k = step(
        either(far_o, jnp.where(at_far, mine[1], y_0)),
        (x_full, across),
        (mine[0], other_x),
        (mine[1], other_y),
        (mine, other_core),
    )
    amp_full, amp_give = amp_part(x, 0, amp_later), amp_part(1 - x, 0, amp_later)
    amp_own, amp_late = amp_part(x, 1, amp_later), amp_part(1 - x, 1, amp_later)
    mixed = [both(give_split, amp_give, i) for i in range(2)]
    before += [amp_full, amp_own, amp_late, *mixed]

    near_x, third_o, x_1, xy_0, first_k = step(
        (x_full, near),
        (near_o, across),
        (mine[1], other_x),
        (x_0, other_y),
        (jnp.stack([y_0, y_1, x_0]), other_core),
    )
    out_x, third_x, mixed[0], xy_1, second_k = step(
        either(far_x, jnp.where(at_far, x_1, xy_0)),
        (near_x, across),
        (mixed[0], other_x),
        (x_1, other_y),
        (jnp.stack([x_1, xy_0]), other_core),
    )
    split = [jnp.stack([o_split[:depth], mixed[0][0]])]
    beside, far_split, third_split = [None, None], [None, None], [None, None]
    beside[0], far_split[0], mixed[1], end_y, xy_k = step(
        (split[0], near),
        (split[0], across),
        (mixed[1], other_x),
        (out_o, between_inner(other_y)),
        (xy_1, other_core),
    )
    lefts = (mine[0], mine[1], x_0, x_1, mine_k[0], mine_k[1], (first_k, 2), (second_k, 0))
    lefts += (y_0, y_1, xy_0, xy_1, (first_k, 0), (first_k, 1), (second_k, 1), xy_k)

    def full(i, total):
        pieces = [(v, i) for v in (o_full, x_full, near_o, near_x, far_o, far_x, third_o, third_x)]
        return add_ladder(pieces, which, lefts, [(amp_full, i), (mixed[i], 1)], total, depth)

    def parted(i, total):
        pieces = [(v, h) for v in (split[i], beside[i], far_split[i], third_split[i]) for h in range(2)]
        return add_ladder(pieces, which, lefts, [(v, i) for v in amp_split], total, depth)

    def far_half(i, from_near, total):
        far = jnp.where(is_inner, far_split[i], both(out_o, out_x, i))
        third = jnp.where(is_inner, third_split[i], from_near)
        amp = jnp.stack([amp_full[i * depth : (i + 1) * depth], mixed[i][1]])
        amp = jnp.where(is_inner, from_near, amp)
        pieces = [(v, h) for v in (far, third) for h in range(2)]
        sets = (*ends, *lefts)
        return add_ladder(pieces, which_far, sets, [(amp, 0), (amp, 1)], total, depth, choices=3)

    total = full(0, None)
    before.append(total)
    split.append(jnp.stack([o_split[depth:], mixed[1][0]]))
    beside[1], third_split[0], amp_late, end_xy, end_k = step(
        (split[1], near),
        (beside[0], across),
        (amp_late, other_x),
        (out_x, between_inner(other_y)),
        (jnp.stack([out_o, out_x]), other_core),
    )
    amp_split = amp_own, amp_late
    total = full(1, total)
    before.append(total)
    amp_both = [both(*now(*amp_split), i) for i in range(2)]
    third_full = [both(third_o, third_x, i) for i in range(2)]
    e7, far_split[1], end_yk = step(
        either(third_full[0], amp_both[0]),
        (split[1], across),
        (jnp.stack([end_y, end_xy]), other_core),
    )
    total = parted(0, total)
    before.append(total)
    e8, third_split[1] = step(either(third_full[1], amp_both[1]), (beside[1], across))
    ends = (out_o, end_y, out_x, end_xy, (end_k, 0), (end_yk, 0), (end_k, 1), (end_yk, 1))
    total = far_half(0, e7, total)
    before.append(total)
    (e8,) = now(e8)
    total = parted(1, total)
    total = far_half(1, e8, total)

    def pick(value, at):
        return lax.dynamic_index_in_dim(value, at, 0, keepdims=False)

    pairs = amplitudes.shape[2]
    own_a, own_pairs = width_a // n_col, pairs // n_row
    total = total.reshape(n_y, 2, own_a, width_b, pairs)
    keep = lax.dynamic_index_in_dim(total, core, 1, keepdims=False)
    give = lax.dynamic_index_in_dim(total, 1 - core, 1, keepdims=False)
    part = keep + send(give, other_core)
    part = part.reshape(n_y, own_a * width_b, n_z, 2, own_pairs).transpose(3, 0, 2, 4, 1)

    def over_x(v):
        return pick(v, x) + send(pick(v, 1 - x), other_x)

    def over_y(v):
        return pick(v, y) + send(pick(v, 1 - y), other_y)

    cut = own_pairs // 2
    first = over_y(over_x(part[:, :, :, :cut]))
    second = over_x(over_y(part[:, :, :, cut:].transpose(1, 0, 2, 3, 4)))
    part = jnp.concatenate([first, second], axis=1)
    ladder = pick(part, z)
    for step in range(1, n_z):
        ladder = ladder + send(pick(part, z ^ step), lambda c, x, y, k, s=step: (c ^ s, x, y, k))
    ladder = ladder.reshape(own_pairs, own_a, width_b)
    denom = eps_left[None, :, None] + eps_right[None, None, :] - pair_energy[:, None, None]
    return ladder / denom


def solution(mesh):
    n_row, n_col = mesh.shape["row"], mesh.shape["col"]
    lines = n_row == 2 * n_col and n_col == 4
    per_device = functools.partial(by_lines, n_row, n_col) if lines else gathered_whole
    in_specs = (
        P(None, "row", "col"),
        P("col", "row"),
        P("row", "col", None),
        P("col"),
        P(),
        P("row"),
    )
    out_specs = P("row", "col", None)
    return jax.shard_map(
        per_device, mesh=mesh, in_specs=in_specs, out_specs=out_specs, check_vma=False
    )
```

```python
import functools

import jax
import jax.numpy as jnp
from jax import lax
from jax.experimental import pallas as pl
from jax.experimental.pallas import tpu as pltpu
from jax.sharding import PartitionSpec as P

AXES = ("row", "col")
PART_A = 4


def contract_aux(left_piece, right_piece):
    return lax.dot_general(
        left_piece, right_piece, (((2,), (1,)), ((), ())), preferred_element_type=jnp.float32
    )


def gathered_whole(left_factors, right_factors, amplitudes, eps_left, eps_right, pair_energy):
    width_a, local_c, _ = left_factors.shape
    local_d = right_factors.shape[0]
    width_b = eps_right.shape[0]
    pairs = amplitudes.shape[2]
    gathered = lax.all_gather(right_factors, "row", axis=1, tiled=True)
    right_whole = gathered.reshape(local_d, -1, width_b)
    left_whole = lax.all_gather(left_factors, "col", axis=2, tiled=True)
    integ = contract_aux(left_whole, right_whole)
    integ = integ.astype(jnp.bfloat16)
    n_row = lax.axis_size("row")
    n_col = lax.axis_size("col")
    own_pairs = pairs // n_row
    own_a = width_a // n_col
    partial_value = jnp.einsum(
        "cdp,acdb->pab", amplitudes, integ, preferred_element_type=jnp.float32
    )
    partial_value = partial_value.reshape(pairs, width_a * width_b)
    section = lax.psum_scatter(partial_value, "row", scatter_dimension=0, tiled=True)
    ladder = lax.psum_scatter(section, "col", scatter_dimension=1, tiled=True)
    ladder = ladder.reshape(own_pairs, own_a, width_b)
    denom = eps_left[None, :, None] + eps_right[None, None, :] - pair_energy[:, None, None]
    return ladder / denom


def ladder_kernel(plans, operands, first, which_ref, *refs):
    inputs, refs = refs[:operands], refs[operands:]
    *add_ref, out_ref = refs[: 1 if first else 2]
    scratch = refs[1 if first else 2 :]
    held_shape = scratch[2].shape
    tile_a, chunk_c, width_q = held_shape[3], held_shape[5], held_shape[6]
    _, depth, width_b, _ = scratch[0].shape
    span = 2 * chunk_c
    step, steps = pl.program_id(0), pl.num_programs(0)
    slot = lax.rem(step, 2)

    def view(entry, rows):
        operand, place = entry
        ref = inputs[operand]
        if rows is None:
            return ref.at[place] if len(ref.shape) == 4 else ref.at[pl.ds(place * depth, depth)]
        return ref.at[rows] if place is None else ref.at[place, rows]

    def whole(group, choice):
        pieces, _, amps = plans[group][choice]
        right, amp, _, sems, _ = scratch[5 * group : 5 * group + 5]
        pairs = [(v, right.at[s]) for s, v in enumerate(pieces)]
        pairs += [(v, amp.at[s]) for s, v in enumerate(amps)]
        return [
            pltpu.make_async_copy(view(v, None), to, sems.at[n]) for n, (v, to) in enumerate(pairs)
        ]

    def tiles(group, choice, at, slot):
        lefts = plans[group][choice][1]
        held, sems = scratch[5 * group + 2], scratch[5 * group + 4]
        rows = pl.ds(pl.multiple_of(at * tile_a, tile_a), tile_a)
        return [
            pltpu.make_async_copy(
                view(lefts[4 * r + 2 * s + h], rows), held.at[slot, r, h, :, s], sems.at[slot, r, h, s]
            )
            for r in range(len(lefts) // 4)
            for h in range(2)
            for s in range(2)
        ]

    ends = []
    for plan in plans:
        ends.append((ends[-1] if ends else 0) + 2 * len(plan[0][0]) + 1)

    def start(group, copies):
        plan = plans[group]
        for choice in range(len(plan)):

            def go():
                for copy in copies(choice):
                    copy.start()

            if len(plan) == 1:
                go()
            else:
                pl.when(which_ref[ends[group] - 1] == choice)(go)

    @pl.when(step == 0)
    def _():
        for group in range(len(plans)):
            start(group, lambda choice: whole(group, choice) + tiles(group, choice, step, 0))

    @pl.when(step + 1 < steps)
    def _():
        for group in range(len(plans)):
            start(group, lambda choice: tiles(group, choice, step + 1, 1 - slot))

    def product(group, rows):
        pieces = plans[group][0][0]
        right, amp, held = scratch[5 * group : 5 * group + 3]
        base = ends[group] - 2 * len(pieces) - 1
        integ = None
        for s in range(len(pieces)):
            left = held[slot, which_ref[base + 2 * s], which_ref[base + 2 * s + 1], rows]
            term = lax.dot_general(
                right[s].reshape(depth * width_b, width_q),
                left.reshape(-1, width_q),
                (((1,), (1,)), ((), ())),
                preferred_element_type=jnp.float32,
            )
            integ = term if integ is None else integ + term
        integ = integ.astype(jnp.bfloat16)
        integ = jnp.concatenate(
            [
                jnp.concatenate(
                    [
                        integ[d * width_b : (d + 1) * width_b, a * span : (a + 1) * span]
                        for d in range(depth)
                    ],
                    axis=1,
                )
                for a in range(integ.shape[1] // span)
            ],
            axis=0,
        )
        both = jnp.concatenate([amp[0], amp[1]], axis=1).reshape(depth * span, -1)
        return jnp.dot(integ, both, preferred_element_type=jnp.float32)

    for group in range(len(plans)):

        @pl.when(step == 0)
        def _():
            for copy in whole(group, 0):
                copy.wait()

        for copy in tiles(group, 0, step, slot):
            copy.wait()
        for at in range(0, tile_a, PART_A):
            rows = slice(at, at + PART_A)
            out = product(group, rows).reshape(PART_A, width_b, -1)
            if group == 0:
                out_ref[rows] = out if first else add_ref[0][rows] + out
            else:
                out_ref[rows] += out


def add_ladder(groups, which, add, depth):
    operands, plans = [], []
    for group in groups:
        plan = []
        for choice in group:
            entries = []
            for part in choice:
                for array, _ in part:
                    if not any(array is v for v in operands):
                        operands.append(array)
                entries.append(
                    [(next(n for n, v in enumerate(operands) if v is a), place) for a, place in part]
                )
            plan.append(entries)
        plans.append(plan)
    pieces, lefts, amps = groups[0][0]
    width_b, width_q = pieces[0][0].shape[-2:]
    width_a, chunk_c = lefts[0][0].shape[-3:-1]
    pairs = amps[0][0].shape[-1]
    tile_a = 2 * PART_A
    scratch, products, moved = [], 0, 8 * width_a * width_b * pairs
    for group in groups:
        slots, n_left = len(group[0][0]), len(group[0][1]) // 4
        scratch += [
            pltpu.VMEM((slots, depth, width_b, width_q), jnp.bfloat16),
            pltpu.VMEM((2, depth, chunk_c, pairs), jnp.bfloat16),
            pltpu.VMEM((2, n_left, 2, tile_a, 2, chunk_c, width_q), jnp.bfloat16),
            pltpu.SemaphoreType.DMA((slots + 2,)),
            pltpu.SemaphoreType.DMA((2, n_left, 2, 2)),
        ]
        products += depth * width_b * width_a * 2 * chunk_c * (slots * width_q + pairs)
        moved += 2 * depth * (slots * width_b * width_q + 2 * chunk_c * pairs)
        moved += 8 * n_left * width_a * chunk_c * width_q
    more = () if add is None else (add,)
    out_spec = pl.BlockSpec((tile_a, width_b, pairs), lambda i, w: (i, 0, 0))
    return pl.pallas_call(
        functools.partial(ladder_kernel, plans, len(operands), add is None),
        grid_spec=pltpu.PrefetchScalarGridSpec(
            num_scalar_prefetch=1,
            grid=(width_a // tile_a,),
            in_specs=[pl.BlockSpec(memory_space=pl.ANY)] * len(operands) + [out_spec] * len(more),
            out_specs=out_spec,
            scratch_shapes=scratch,
        ),
        out_shape=jax.ShapeDtypeStruct((width_a, width_b, pairs), jnp.float32),
        input_output_aliases={len(operands) + 1: 0} if more else {},
        cost_estimate=pl.CostEstimate(flops=2 * products, bytes_accessed=moved, transcendentals=0),
        compiler_params=pltpu.CompilerParams(vmem_limit_bytes=44 * 2**20),
        name="ladder",
    )(which, *operands, *more)


def by_lines(n_row, n_col, *arrays):
    left_factors, right_factors, amplitudes, eps_left, eps_right, pair_energy = arrays
    row, col = lax.axis_index("row"), lax.axis_index("col")
    n_z, n_y = n_row // 2, n_col // 2
    z, x, y, core = row // 2, row % 2, col // 2, col % 2
    half = n_z // 2

    def inner(at):
        return at in (half - 1, half)

    before = []

    def send(value, place):
        pairs = []
        for at_z in range(n_z):
            for at_x in range(2):
                for at_y in range(n_y):
                    for at_k in range(2):
                        to = place(at_z, at_x, at_y, at_k)
                        if to is not None:
                            source = (at_z * 2 + at_x) * n_col + at_y * 2 + at_k
                            target = (to[0] * 2 + to[1]) * n_col + to[2] * 2 + to[3]
                            pairs.append((source, target))
        return lax.ppermute(value, AXES, pairs)

    def now(*values):
        return lax.optimization_barrier((values, tuple(before)))[0]

    def step(*transfers, beside=()):
        values = now(*(value for value, _ in transfers))
        got = [send(value, place) for value, (_, place) in zip(values, transfers)]
        before[:] = [*got, *beside]
        return got

    def other_x(c, x, y, k):
        return c, 1 - x, y, k

    def other_y(c, x, y, k):
        return c, x, 1 - y, k

    def other_core(c, x, y, k):
        return c, x, y, 1 - k

    def near(c, x, y, k):
        return c ^ 1, x, y, k

    def across(c, x, y, k):
        return (n_z - 1 - c, x, y, k) if inner(c) else None

    def outward(c, x, y, k):
        return (c ^ 1, x, y, k) if inner(c) else None

    def between_inner(step):
        return lambda c, x, y, k: step(c, x, y, k) if inner(c) else None

    is_inner = (z == half - 1) | (z == half)
    at_far = y == 1 - z // half

    width_a, local_c, local_q = left_factors.shape
    mine = left_factors.reshape(width_a, local_c, 2, local_q // 2).transpose(2, 0, 1, 3)

    local_d = right_factors.shape[0]
    width_b = eps_right.shape[0]
    part_d = local_d // 4
    depth = part_d // 2

    def right_part(at_x, part, right=right_factors):
        rows = lax.dynamic_slice_in_dim(right, at_x * 2 * part_d + part * part_d, part_d)
        return rows.reshape(part_d, -1, width_b).transpose(0, 2, 1)

    def amp_part(at_x, part, amp):
        got = lax.dynamic_slice_in_dim(amp, at_x * 2 * part_d + part * part_d, part_d, 1)
        return got.transpose(1, 0, 2)

    def both(one, two, at):
        rows = slice(at * depth, (at + 1) * depth)
        return jnp.stack([one[rows], two[rows]])

    def either(inner_one, end_one):
        return jnp.where(is_inner, inner_one, end_one.reshape(inner_one.shape)), near

    far_inner = jnp.where(z < half, half, half - 1)
    planes = (z, z ^ 1, far_inner, far_inner ^ 1)
    which = jnp.stack([v for p in planes for v in (p ^ col, x, p ^ col, 1 - x)] + [jnp.zeros_like(x)])
    turn = jnp.where(is_inner & at_far, 1, 0)
    choice = jnp.where(is_inner, 0, jnp.where(at_far, 1, 2))
    which_far = [v for p in planes[2:] for v in ((p % 2) ^ core, x ^ turn, (p % 2) ^ core, 1 - x ^ turn)]
    which_far = jnp.stack(which_far + [choice])

    mine, x_give, o_full = lax.optimization_barrier((mine, right_part(1 - x, 0), right_part(x, 0)))
    before[:] = [x_give, o_full]
    (right_later,) = now(right_factors)
    near_o, far_o, x_full, y_0 = step(
        (o_full, near), (o_full, across), (x_give, other_x), (mine[0], other_y)
    )
    give_split, o_split = right_part(1 - x, 1, right_later), right_part(x, 1, right_later)
    before += [give_split, o_split]

    (amp_later,) = now(amplitudes)
    out_o, far_x, x_0, y_1, mine_k = step(
        either(far_o, jnp.where(at_far, mine[1], y_0)),
        (x_full, across),
        (mine[0], other_x),
        (mine[1], other_y),
        (mine, other_core),
    )
    amp_full, amp_give = amp_part(x, 0, amp_later), amp_part(1 - x, 0, amp_later)
    amp_own, amp_late = amp_part(x, 1, amp_later), amp_part(1 - x, 1, amp_later)
    mixed = [both(give_split, amp_give, i) for i in range(2)]
    before += [amp_full, amp_own, amp_late, *mixed]

    near_x, third_o, x_1, xy_0, first_k = step(
        (x_full, near),
        (near_o, across),
        (mine[1], other_x),
        (x_0, other_y),
        (jnp.stack([y_0, y_1, x_0]), other_core),
    )
    out_x, third_x, mixed[0], xy_1, second_k = step(
        either(far_x, jnp.where(at_far, x_1, xy_0)),
        (near_x, across),
        (mixed[0], other_x),
        (x_1, other_y),
        (jnp.stack([x_1, xy_0]), other_core),
    )
    split = [jnp.stack([o_split[:depth], mixed[0][0]])]
    beside, far_split, third_split = [None, None], [None, None], [None, None]
    beside[0], far_split[0], mixed[1], end_y, xy_k = step(
        (split[0], near),
        (split[0], across),
        (mixed[1], other_x),
        (out_o, between_inner(other_y)),
        (xy_1, other_core),
    )
    mine_0, mine_1 = mine[0], mine[1]
    lefts = [(mine_0, None), (mine_1, None), (x_0, None), (x_1, None)]
    lefts += [(mine_k, 0), (mine_k, 1), (first_k, 2), (second_k, 0)]
    lefts += [(y_0, None), (y_1, None), (xy_0, None), (xy_1, None)]
    lefts += [(first_k, 0), (first_k, 1), (second_k, 1), (xy_k, None)]

    def full(i):
        pieces = [(v, i) for v in (o_full, x_full, near_o, near_x, far_o, far_x, third_o, third_x)]
        return [(pieces, lefts, [(amp_full, i), (mixed[i], 1)])]

    def parted(i):
        pieces = [(v, h) for v in (split[i], beside[i], far_split[i], third_split[i]) for h in range(2)]
        return [(pieces, lefts, [(amp_own, i), (amp_late, i)])]

    def far_half(i, from_near):
        ends = [(out_o, None), (end_y, None), (out_x, None), (end_xy, None)]
        ends += [(end_k, 0), (end_yk, 0), (end_k, 1), (end_yk, 1)]
        got = [(from_near, 0), (from_near, 1)]
        pieces = [(v, h) for v in (far_split[i], third_split[i]) for h in range(2)]
        own = [(out_o, i), (out_x, i), *got], [(amp_full, i), (mixed[i], 1)]
        return [(pieces, ends, got), *((own[0], v, own[1]) for v in (lefts[:8], lefts[8:]))]

    total = add_ladder([full(0)], which, None, depth)
    before.append(total)
    mixed[1], third_o, third_x = now(mixed[1], third_o, third_x)
    split.append(jnp.stack([o_split[depth:], mixed[1][0]]))
    beside[1], third_split[0], amp_late, end_xy, end_k = step(
        (split[1], near),
        (beside[0], across),
        (amp_late, other_x),
        (out_x, between_inner(other_y)),
        (jnp.stack([out_o, out_x]), other_core),
    )
    total = add_ladder([full(1)], which, total, depth)
    before.append(total)
    amp_own, amp_late, third_o, third_x, end_y, end_xy = now(
        amp_own, amp_late, third_o, third_x, end_y, end_xy
    )
    e7, far_split[1], end_yk = step(
        either(both(third_o, third_x, 0), both(amp_own, amp_late, 0)),
        (split[1], across),
        (jnp.stack([end_y, end_xy]), other_core),
    )
    total = add_ladder([parted(0)], which, total, depth)
    before.append(total)
    third_o, third_x, amp_own, amp_late = now(third_o, third_x, amp_own, amp_late)
    e8, third_split[1] = step(
        either(both(third_o, third_x, 1), both(amp_own, amp_late, 1)), (beside[1], across)
    )
    total = add_ladder([far_half(0, e7)], which_far, total, depth)
    before.append(total)
    e8, third_split[1] = now(e8, third_split[1])
    total = add_ladder([parted(1)], which, total, depth)
    total = add_ladder([far_half(1, e8)], which_far, total, depth)

    def pick(value, at):
        return lax.dynamic_index_in_dim(value, at, 0, keepdims=False)

    pairs = amplitudes.shape[2]
    own_a, own_pairs = width_a // n_col, pairs // n_row
    total = total.reshape(n_y, 2, own_a, width_b, pairs)
    keep = lax.dynamic_index_in_dim(total, core, 1, keepdims=False)
    give = lax.dynamic_index_in_dim(total, 1 - core, 1, keepdims=False)
    part = keep + send(give, other_core)
    part = part.reshape(n_y, own_a * width_b, n_z, 2, own_pairs).transpose(3, 0, 2, 4, 1)

    def over_x(v):
        return pick(v, x) + send(pick(v, 1 - x), other_x)

    def over_y(v):
        return pick(v, y) + send(pick(v, 1 - y), other_y)

    cut = own_pairs // 2
    first = over_y(over_x(part[:, :, :, :cut]))
    second = over_x(over_y(part[:, :, :, cut:].transpose(1, 0, 2, 3, 4)))
    part = jnp.concatenate([first, second], axis=1)
    ladder = pick(part, z)
    for step in range(1, n_z):
        ladder = ladder + send(pick(part, z ^ step), lambda c, x, y, k, s=step: (c ^ s, x, y, k))
    ladder = ladder.reshape(own_pairs, own_a, width_b)
    denom = eps_left[None, :, None] + eps_right[None, None, :] - pair_energy[:, None, None]
    return ladder / denom


def solution(mesh):
    n_row, n_col = mesh.shape["row"], mesh.shape["col"]
    lines = n_row == 2 * n_col and n_col == 4
    per_device = functools.partial(by_lines, n_row, n_col) if lines else gathered_whole
    in_specs = (
        P(None, "row", "col"),
        P("col", "row"),
        P("row", "col", None),
        P("col"),
        P(),
        P("row"),
    )
    out_specs = P("row", "col", None)
    return jax.shard_map(
        per_device, mesh=mesh, in_specs=in_specs, out_specs=out_specs, check_vma=False
    )
```

```python
import functools

import jax
import jax.numpy as jnp
from jax import lax
from jax.experimental import pallas as pl
from jax.experimental.pallas import tpu as pltpu
from jax.sharding import PartitionSpec as P

AXES = ("row", "col")
PART_A = 4


def contract_aux(left_piece, right_piece):
    return lax.dot_general(
        left_piece, right_piece, (((2,), (1,)), ((), ())), preferred_element_type=jnp.float32
    )


def gathered_whole(left_factors, right_factors, amplitudes, eps_left, eps_right, pair_energy):
    width_a, local_c, _ = left_factors.shape
    local_d = right_factors.shape[0]
    width_b = eps_right.shape[0]
    pairs = amplitudes.shape[2]
    gathered = lax.all_gather(right_factors, "row", axis=1, tiled=True)
    right_whole = gathered.reshape(local_d, -1, width_b)
    left_whole = lax.all_gather(left_factors, "col", axis=2, tiled=True)
    integ = contract_aux(left_whole, right_whole)
    integ = integ.astype(jnp.bfloat16)
    n_row = lax.axis_size("row")
    n_col = lax.axis_size("col")
    own_pairs = pairs // n_row
    own_a = width_a // n_col
    partial_value = jnp.einsum(
        "cdp,acdb->pab", amplitudes, integ, preferred_element_type=jnp.float32
    )
    partial_value = partial_value.reshape(pairs, width_a * width_b)
    section = lax.psum_scatter(partial_value, "row", scatter_dimension=0, tiled=True)
    ladder = lax.psum_scatter(section, "col", scatter_dimension=1, tiled=True)
    ladder = ladder.reshape(own_pairs, own_a, width_b)
    denom = eps_left[None, :, None] + eps_right[None, None, :] - pair_energy[:, None, None]
    return ladder / denom


def ladder_kernel(plans, operands, first, last, which_ref, *refs):
    inputs, refs = refs[:operands], refs[operands:]
    *add_ref, out_ref = refs[: 1 if first else 2]
    scratch = refs[1 if first else 2 :]
    held_shape = scratch[2].shape
    tile_a, chunk_c, width_q = held_shape[3], held_shape[5], held_shape[6]
    _, depth, width_b, _ = scratch[0].shape
    span = 2 * chunk_c
    step, steps = pl.program_id(0), pl.num_programs(0)
    slot = lax.rem(step, 2)

    def view(entry, rows):
        operand, place = entry
        ref = inputs[operand]
        if rows is None:
            return ref.at[place] if len(ref.shape) == 4 else ref.at[pl.ds(place * depth, depth)]
        return ref.at[rows] if place is None else ref.at[place, rows]

    def whole(group, choice):
        pieces, _, amps = plans[group][choice]
        right, amp, _, sems, _ = scratch[5 * group : 5 * group + 5]
        pairs = [(v, right.at[s]) for s, v in enumerate(pieces)]
        pairs += [(v, amp.at[:, s]) for s, v in enumerate(amps)]
        return [
            pltpu.make_async_copy(view(v, None), to, sems.at[n]) for n, (v, to) in enumerate(pairs)
        ]

    def tiles(group, choice, at, slot):
        lefts = plans[group][choice][1]
        held, sems = scratch[5 * group + 2], scratch[5 * group + 4]
        rows = pl.ds(pl.multiple_of(at * tile_a, tile_a), tile_a)
        return [
            pltpu.make_async_copy(
                view(lefts[4 * r + 2 * s + h], rows), held.at[slot, r, h, :, s], sems.at[slot, r, h, s]
            )
            for r in range(len(lefts) // 4)
            for h in range(2)
            for s in range(2)
        ]

    ends = []
    for plan in plans:
        ends.append((ends[-1] if ends else 0) + 2 * len(plan[0][0]) + 1)

    def start(group, copies):
        plan = plans[group]
        for choice in range(len(plan)):

            def go():
                for copy in copies(choice):
                    copy.start()

            if len(plan) == 1:
                go()
            else:
                pl.when(which_ref[ends[group] - 1] == choice)(go)

    @pl.when(step == 0)
    def _():
        for group in range(len(plans)):
            start(group, lambda choice: whole(group, choice) + tiles(group, choice, step, 0))

    @pl.when(step + 1 < steps)
    def _():
        for group in range(len(plans)):
            start(group, lambda choice: tiles(group, choice, step + 1, 1 - slot))

    def product(group, rows):
        pieces = plans[group][0][0]
        right, amp, held = scratch[5 * group : 5 * group + 3]
        base = ends[group] - 2 * len(pieces) - 1
        integ = None
        for s in range(len(pieces)):
            left = held[slot, which_ref[base + 2 * s], which_ref[base + 2 * s + 1], rows]
            term = lax.dot_general(
                right[s].reshape(depth * width_b, width_q),
                left.reshape(-1, width_q),
                (((1,), (1,)), ((), ())),
                preferred_element_type=jnp.float32,
            )
            integ = term if integ is None else integ + term
        integ = integ.astype(jnp.bfloat16)
        integ = jnp.concatenate(
            [
                jnp.concatenate(
                    [
                        integ[d * width_b : (d + 1) * width_b, a * span : (a + 1) * span]
                        for d in range(depth)
                    ],
                    axis=1,
                )
                for a in range(integ.shape[1] // span)
            ],
            axis=0,
        )
        both = amp[...].reshape(depth * span, -1)
        return jnp.dot(integ, both, preferred_element_type=jnp.float32)

    for group in range(len(plans)):

        @pl.when(step == 0)
        def _():
            for copy in whole(group, 0):
                copy.wait()

        for copy in tiles(group, 0, step, slot):
            copy.wait()
        for at in range(0, tile_a, PART_A):
            rows = slice(at, at + PART_A)
            out = product(group, rows).reshape(PART_A, width_b, -1)
            out = out if first else add_ref[0][rows] + out
            if last:
                out_ref[:, at * width_b : (at + PART_A) * width_b] = out.reshape(-1, out.shape[-1]).T
            else:
                out_ref[rows] = out


def add_ladder(groups, which, add, depth, last=False, vmem=44):
    operands, plans = [], []
    for group in groups:
        plan = []
        for choice in group:
            entries = []
            for part in choice:
                for array, _ in part:
                    if not any(array is v for v in operands):
                        operands.append(array)
                entries.append(
                    [(next(n for n, v in enumerate(operands) if v is a), place) for a, place in part]
                )
            plan.append(entries)
        plans.append(plan)
    pieces, lefts, amps = groups[0][0]
    width_b, width_q = pieces[0][0].shape[-2:]
    width_a, chunk_c = lefts[0][0].shape[-3:-1]
    pairs = amps[0][0].shape[-1]
    tile_a = 2 * PART_A
    scratch, products, moved = [], 0, 8 * width_a * width_b * pairs
    for group in groups:
        slots, n_left = len(group[0][0]), len(group[0][1]) // 4
        scratch += [
            pltpu.VMEM((slots, depth, width_b, width_q), jnp.bfloat16),
            pltpu.VMEM((depth, 2, chunk_c, pairs), jnp.bfloat16),
            pltpu.VMEM((2, n_left, 2, tile_a, 2, chunk_c, width_q), jnp.bfloat16),
            pltpu.SemaphoreType.DMA((slots + 2,)),
            pltpu.SemaphoreType.DMA((2, n_left, 2, 2)),
        ]
        products += depth * width_b * width_a * 2 * chunk_c * (slots * width_q + pairs)
        moved += 2 * depth * (slots * width_b * width_q + 2 * chunk_c * pairs)
        moved += 8 * n_left * width_a * chunk_c * width_q
    more = () if add is None else (add,)
    add_spec = pl.BlockSpec((tile_a, width_b, pairs), lambda i, w: (i, 0, 0))
    if last:
        shape = (width_a // tile_a, pairs, tile_a * width_b)
        out_spec = pl.BlockSpec((None, *shape[1:]), lambda i, w: (i, 0, 0))
    else:
        shape, out_spec = (width_a, width_b, pairs), add_spec
    return pl.pallas_call(
        functools.partial(ladder_kernel, plans, len(operands), add is None, last),
        grid_spec=pltpu.PrefetchScalarGridSpec(
            num_scalar_prefetch=1,
            grid=(width_a // tile_a,),
            in_specs=[pl.BlockSpec(memory_space=pl.ANY)] * len(operands) + [add_spec] * len(more),
            out_specs=out_spec,
            scratch_shapes=scratch,
        ),
        out_shape=jax.ShapeDtypeStruct(shape, jnp.float32),
        input_output_aliases={len(operands) + 1: 0} if more and not last else {},
        cost_estimate=pl.CostEstimate(flops=2 * products, bytes_accessed=moved, transcendentals=0),
        compiler_params=pltpu.CompilerParams(vmem_limit_bytes=vmem * 2**20),
        name="ladder",
    )(which, *operands, *more)


def by_lines(n_row, n_col, *arrays):
    left_factors, right_factors, amplitudes, eps_left, eps_right, pair_energy = arrays
    row, col = lax.axis_index("row"), lax.axis_index("col")
    n_z, n_y = n_row // 2, n_col // 2
    z, x, y, core = row // 2, row % 2, col // 2, col % 2
    half = n_z // 2

    def inner(at):
        return at in (half - 1, half)

    before = []

    def send(value, place):
        pairs = []
        for at_z in range(n_z):
            for at_x in range(2):
                for at_y in range(n_y):
                    for at_k in range(2):
                        to = place(at_z, at_x, at_y, at_k)
                        if to is not None:
                            source = (at_z * 2 + at_x) * n_col + at_y * 2 + at_k
                            target = (to[0] * 2 + to[1]) * n_col + to[2] * 2 + to[3]
                            pairs.append((source, target))
        return lax.ppermute(value, AXES, pairs)

    def now(*values):
        return lax.optimization_barrier((values, tuple(before)))[0]

    def step(*transfers, beside=()):
        values = now(*(value for value, _ in transfers))
        got = [send(value, place) for value, (_, place) in zip(values, transfers)]
        before[:] = [*got, *beside]
        return got

    def other_x(c, x, y, k):
        return c, 1 - x, y, k

    def other_y(c, x, y, k):
        return c, x, 1 - y, k

    def other_core(c, x, y, k):
        return c, x, y, 1 - k

    def near(c, x, y, k):
        return c ^ 1, x, y, k

    def across(c, x, y, k):
        return (n_z - 1 - c, x, y, k) if inner(c) else None

    def outward(c, x, y, k):
        return (c ^ 1, x, y, k) if inner(c) else None

    def between_inner(step):
        return lambda c, x, y, k: step(c, x, y, k) if inner(c) else None

    is_inner = (z == half - 1) | (z == half)
    at_far = y == 1 - z // half

    width_a, local_c, local_q = left_factors.shape
    mine = left_factors.reshape(width_a, local_c, 2, local_q // 2).transpose(2, 0, 1, 3)

    local_d = right_factors.shape[0]
    width_b = eps_right.shape[0]
    part_d = local_d // 4
    depth = part_d // 2

    def right_part(at_x, part, right=right_factors):
        rows = lax.dynamic_slice_in_dim(right, at_x * 2 * part_d + part * part_d, part_d)
        return rows.reshape(part_d, -1, width_b).transpose(0, 2, 1)

    def amp_part(at_x, part, amp):
        got = lax.dynamic_slice_in_dim(amp, at_x * 2 * part_d + part * part_d, part_d, 1)
        return got.transpose(1, 0, 2)

    def both(one, two, at):
        rows = slice(at * depth, (at + 1) * depth)
        return jnp.stack([one[rows], two[rows]])

    def either(inner_one, end_one):
        return jnp.where(is_inner, inner_one, end_one.reshape(inner_one.shape)), near

    far_inner = jnp.where(z < half, half, half - 1)
    planes = (z, z ^ 1, far_inner, far_inner ^ 1)
    which = jnp.stack([v for p in planes for v in (p ^ col, x, p ^ col, 1 - x)] + [jnp.zeros_like(x)])
    turn = jnp.where(is_inner & at_far, 1, 0)
    choice = jnp.where(is_inner, 0, jnp.where(at_far, 1, 2))
    which_far = [v for p in planes[2:] for v in ((p % 2) ^ core, x ^ turn, (p % 2) ^ core, 1 - x ^ turn)]
    which_far = jnp.stack(which_far + [choice])

    mine, x_give, o_full = lax.optimization_barrier((mine, right_part(1 - x, 0), right_part(x, 0)))
    before[:] = [x_give, o_full]
    (right_later,) = now(right_factors)
    near_o, far_o, x_full, y_0 = step(
        (o_full, near), (o_full, across), (x_give, other_x), (mine[0], other_y)
    )
    give_split, o_split = right_part(1 - x, 1, right_later), right_part(x, 1, right_later)
    before += [give_split, o_split]

    (amp_later,) = now(amplitudes)
    out_o, far_x, x_0, y_1, mine_k = step(
        either(far_o, jnp.where(at_far, mine[1], y_0)),
        (x_full, across),
        (mine[0], other_x),
        (mine[1], other_y),
        (mine, other_core),
    )
    amp_full, amp_give = amp_part(x, 0, amp_later), amp_part(1 - x, 0, amp_later)
    amp_own, amp_late = amp_part(x, 1, amp_later), amp_part(1 - x, 1, amp_later)
    mixed = [both(give_split, amp_give, i) for i in range(2)]
    before += [amp_full, amp_own, amp_late, *mixed]

    near_x, third_o, x_1, xy_0, first_k = step(
        (x_full, near),
        (near_o, across),
        (mine[1], other_x),
        (x_0, other_y),
        (jnp.stack([y_0, y_1, x_0]), other_core),
    )
    out_x, third_x, mixed[0], xy_1, second_k = step(
        either(far_x, jnp.where(at_far, x_1, xy_0)),
        (near_x, across),
        (mixed[0], other_x),
        (x_1, other_y),
        (jnp.stack([x_1, xy_0]), other_core),
    )
    split = [jnp.stack([o_split[:depth], mixed[0][0]])]
    beside, far_split, third_split = [None, None], [None, None], [None, None]
    beside[0], far_split[0], mixed[1], end_y, xy_k = step(
        (split[0], near),
        (split[0], across),
        (mixed[1], other_x),
        (out_o, between_inner(other_y)),
        (xy_1, other_core),
    )
    mine_0, mine_1 = mine[0], mine[1]
    lefts = [(mine_0, None), (mine_1, None), (x_0, None), (x_1, None)]
    lefts += [(mine_k, 0), (mine_k, 1), (first_k, 2), (second_k, 0)]
    lefts += [(y_0, None), (y_1, None), (xy_0, None), (xy_1, None)]
    lefts += [(first_k, 0), (first_k, 1), (second_k, 1), (xy_k, None)]

    def full(i):
        pieces = [(v, i) for v in (o_full, x_full, near_o, near_x, far_o, far_x, third_o, third_x)]
        return [(pieces, lefts, [(amp_full, i), (mixed[i], 1)])]

    def parted(i):
        pieces = [(v, h) for v in (split[i], beside[i], far_split[i], third_split[i]) for h in range(2)]
        return [(pieces, lefts, [(amp_own, i), (amp_late, i)])]

    def far_half(i, from_near):
        ends = [(out_o, None), (end_y, None), (out_x, None), (end_xy, None)]
        ends += [(end_k, 0), (end_yk, 0), (end_k, 1), (end_yk, 1)]
        got = [(from_near, 0), (from_near, 1)]
        pieces = [(v, h) for v in (far_split[i], third_split[i]) for h in range(2)]
        own = [(out_o, i), (out_x, i), *got], [(amp_full, i), (mixed[i], 1)]
        return [(pieces, ends, got), *((own[0], v, own[1]) for v in (lefts[:8], lefts[8:]))]

    total = add_ladder([full(0)], which, None, depth)
    before.append(total)
    mixed[1], third_o, third_x = now(mixed[1], third_o, third_x)
    split.append(jnp.stack([o_split[depth:], mixed[1][0]]))
    beside[1], third_split[0], amp_late, end_xy, far_split[1] = step(
        (split[1], near),
        (beside[0], across),
        (amp_late, other_x),
        (out_x, between_inner(other_y)),
        (split[1], across),
    )
    del before[-1]
    total = add_ladder([full(1)], which, total, depth)
    before.append(total)
    amp_own, amp_late, third_o, third_x, end_y, end_xy = now(
        amp_own, amp_late, third_o, third_x, end_y, end_xy
    )
    e7, third_split[1], end_yk, end_k = step(
        either(both(third_o, third_x, 0), both(amp_own, amp_late, 0)),
        (beside[1], across),
        (jnp.stack([end_y, end_xy]), other_core),
        (jnp.stack([out_o, out_x]), other_core),
    )
    del before[1]
    total = add_ladder([parted(0)], which, total, depth)
    before.append(total)
    third_o, third_x, amp_own, amp_late = now(third_o, third_x, amp_own, amp_late)
    (e8,) = step(either(both(third_o, third_x, 1), both(amp_own, amp_late, 1)))
    total = add_ladder([far_half(0, e7)], which_far, total, depth)
    total = add_ladder([parted(1)], which, total, depth)
    total = add_ladder([far_half(1, e8)], which_far, total, depth, True)

    def pick(value, at):
        return lax.dynamic_index_in_dim(value, at, 0, keepdims=False)

    pairs = amplitudes.shape[2]
    own_a, own_pairs = width_a // n_col, pairs // n_row
    total = total.reshape(n_y, 2, pairs, own_a * width_b)
    keep = lax.dynamic_index_in_dim(total, core, 1, keepdims=False)
    give = lax.dynamic_index_in_dim(total, 1 - core, 1, keepdims=False)
    part = keep + send(give, other_core)
    part = part.reshape(n_y, n_z, 2, own_pairs, own_a * width_b)

    def over_x(v):
        own, other = (lax.dynamic_index_in_dim(v, at, -3, keepdims=False) for at in (x, 1 - x))
        return own + send(other, other_x)

    def over_y(v):
        return pick(v, y) + send(pick(v, 1 - y), other_y)

    cut = own_pairs // 2
    first = over_y(over_x(part[..., :cut, :]))
    second = over_x(over_y(part[..., cut:, :]))
    part = jnp.concatenate([first, second], axis=1)
    ladder = pick(part, z)
    for step in range(1, n_z):
        ladder = ladder + send(pick(part, z ^ step), lambda c, x, y, k, s=step: (c ^ s, x, y, k))
    ladder = ladder.reshape(own_pairs, own_a, width_b)
    denom = eps_left[None, :, None] + eps_right[None, None, :] - pair_energy[:, None, None]
    return ladder / denom


def solution(mesh):
    n_row, n_col = mesh.shape["row"], mesh.shape["col"]
    lines = n_row == 2 * n_col and n_col == 4
    per_device = functools.partial(by_lines, n_row, n_col) if lines else gathered_whole
    in_specs = (
        P(None, "row", "col"),
        P("col", "row"),
        P("row", "col", None),
        P("col"),
        P(),
        P("row"),
    )
    out_specs = P("row", "col", None)
    return jax.shard_map(
        per_device, mesh=mesh, in_specs=in_specs, out_specs=out_specs, check_vma=False
    )
```

```python
import functools

import jax
import jax.numpy as jnp
from jax import lax
from jax.experimental import pallas as pl
from jax.experimental.pallas import tpu as pltpu
from jax.sharding import PartitionSpec as P

AXES = ("row", "col")
PART_A = 4


def contract_aux(left_piece, right_piece):
    return lax.dot_general(
        left_piece, right_piece, (((2,), (1,)), ((), ())), preferred_element_type=jnp.float32
    )


def gathered_whole(left_factors, right_factors, amplitudes, eps_left, eps_right, pair_energy):
    width_a, local_c, _ = left_factors.shape
    local_d = right_factors.shape[0]
    width_b = eps_right.shape[0]
    pairs = amplitudes.shape[2]
    gathered = lax.all_gather(right_factors, "row", axis=1, tiled=True)
    right_whole = gathered.reshape(local_d, -1, width_b)
    left_whole = lax.all_gather(left_factors, "col", axis=2, tiled=True)
    integ = contract_aux(left_whole, right_whole)
    integ = integ.astype(jnp.bfloat16)
    n_row = lax.axis_size("row")
    n_col = lax.axis_size("col")
    own_pairs = pairs // n_row
    own_a = width_a // n_col
    partial_value = jnp.einsum(
        "cdp,acdb->pab", amplitudes, integ, preferred_element_type=jnp.float32
    )
    partial_value = partial_value.reshape(pairs, width_a * width_b)
    section = lax.psum_scatter(partial_value, "row", scatter_dimension=0, tiled=True)
    ladder = lax.psum_scatter(section, "col", scatter_dimension=1, tiled=True)
    ladder = ladder.reshape(own_pairs, own_a, width_b)
    denom = eps_left[None, :, None] + eps_right[None, None, :] - pair_energy[:, None, None]
    return ladder / denom


def ladder_kernel(plans, operands, first, last, parts, which_ref, *refs):
    inputs, refs = refs[:operands], refs[operands:]
    *add_ref, out_ref = refs[: 1 if first else 2]
    scratch = refs[1 if first else 2 :]
    held_shape = scratch[2].shape
    tile_a, chunk_c, width_q = held_shape[3], held_shape[5], held_shape[6]
    _, depth, width_b, _ = scratch[0].shape
    span, sub = 2 * chunk_c, depth // parts
    step, steps = pl.program_id(0), pl.num_programs(0)
    slot = lax.rem(step, 2)

    def view(entry, rows):
        operand, place = entry
        ref = inputs[operand]
        if rows is None:
            return ref.at[place] if len(ref.shape) == 4 else ref.at[pl.ds(place * sub, sub)]
        return ref.at[rows] if place is None else ref.at[place, rows]

    def whole(group, choice):
        pieces, _, amps = plans[group][choice]
        right, amp, _, sems, _ = scratch[5 * group : 5 * group + 5]
        at = [(n // parts, pl.ds(n % parts * sub, sub)) for n in range(len(pieces))]
        pairs = [(v, right.at[s, rows]) for v, (s, rows) in zip(pieces, at)]
        pairs += [(v, amp.at[rows, s]) for v, (s, rows) in zip(amps, at)]
        return [
            pltpu.make_async_copy(view(v, None), to, sems.at[n]) for n, (v, to) in enumerate(pairs)
        ]

    def tiles(group, choice, at, slot):
        lefts = plans[group][choice][1]
        held, sems = scratch[5 * group + 2], scratch[5 * group + 4]
        rows = pl.ds(pl.multiple_of(at * tile_a, tile_a), tile_a)
        return [
            pltpu.make_async_copy(
                view(lefts[4 * r + 2 * s + h], rows), held.at[slot, r, h, :, s], sems.at[slot, r, h, s]
            )
            for r in range(len(lefts) // 4)
            for h in range(2)
            for s in range(2)
        ]

    ends = []
    for plan in plans:
        ends.append((ends[-1] if ends else 0) + 2 * len(plan[0][0]) // parts + 1)

    def start(group, copies):
        plan = plans[group]
        for choice in range(len(plan)):

            def go():
                for copy in copies(choice):
                    copy.start()

            if len(plan) == 1:
                go()
            else:
                pl.when(which_ref[ends[group] - 1] == choice)(go)

    @pl.when(step == 0)
    def _():
        for group in range(len(plans)):
            start(group, lambda choice: whole(group, choice) + tiles(group, choice, step, 0))

    @pl.when(step + 1 < steps)
    def _():
        for group in range(len(plans)):
            start(group, lambda choice: tiles(group, choice, step + 1, 1 - slot))

    def product(group, rows):
        slots = len(plans[group][0][0]) // parts
        right, amp, held = scratch[5 * group : 5 * group + 3]
        base = ends[group] - 2 * slots - 1
        integ = None
        for s in range(slots):
            left = held[slot, which_ref[base + 2 * s], which_ref[base + 2 * s + 1], rows]
            term = lax.dot_general(
                right[s].reshape(depth * width_b, width_q),
                left.reshape(-1, width_q),
                (((1,), (1,)), ((), ())),
                preferred_element_type=jnp.float32,
            )
            integ = term if integ is None else integ + term
        integ = integ.astype(jnp.bfloat16)
        integ = jnp.concatenate(
            [
                jnp.concatenate(
                    [
                        integ[d * width_b : (d + 1) * width_b, a * span : (a + 1) * span]
                        for d in range(depth)
                    ],
                    axis=1,
                )
                for a in range(integ.shape[1] // span)
            ],
            axis=0,
        )
        both = amp[...].reshape(depth * span, -1)
        return jnp.dot(integ, both, preferred_element_type=jnp.float32)

    for group in range(len(plans)):

        @pl.when(step == 0)
        def _():
            for copy in whole(group, 0):
                copy.wait()

        for copy in tiles(group, 0, step, slot):
            copy.wait()
        for at in range(0, tile_a, PART_A):
            rows = slice(at, at + PART_A)
            out = product(group, rows).reshape(PART_A, width_b, -1)
            out = out if first else add_ref[0][rows] + out
            if last:
                out_ref[:, at * width_b : (at + PART_A) * width_b] = out.reshape(-1, out.shape[-1]).T
            else:
                out_ref[rows] = out


def add_ladder(groups, which, add, depth, last=False, vmem=44, parts=1):
    operands, plans = [], []
    depth *= parts
    for group in groups:
        plan = []
        for choice in group:
            entries = []
            for part in choice:
                for array, _ in part:
                    if not any(array is v for v in operands):
                        operands.append(array)
                entries.append(
                    [(next(n for n, v in enumerate(operands) if v is a), place) for a, place in part]
                )
            plan.append(entries)
        plans.append(plan)
    pieces, lefts, amps = groups[0][0]
    width_b, width_q = pieces[0][0].shape[-2:]
    width_a, chunk_c = lefts[0][0].shape[-3:-1]
    pairs = amps[0][0].shape[-1]
    tile_a = 2 * PART_A
    scratch, products, moved = [], 0, 8 * width_a * width_b * pairs
    for group in groups:
        slots, n_left = len(group[0][0]) // parts, len(group[0][1]) // 4
        scratch += [
            pltpu.VMEM((slots, depth, width_b, width_q), jnp.bfloat16),
            pltpu.VMEM((depth, 2, chunk_c, pairs), jnp.bfloat16),
            pltpu.VMEM((2, n_left, 2, tile_a, 2, chunk_c, width_q), jnp.bfloat16),
            pltpu.SemaphoreType.DMA(((slots + 2) * parts,)),
            pltpu.SemaphoreType.DMA((2, n_left, 2, 2)),
        ]
        products += depth * width_b * width_a * 2 * chunk_c * (slots * width_q + pairs)
        moved += 2 * depth * (slots * width_b * width_q + 2 * chunk_c * pairs)
        moved += 8 * n_left * width_a * chunk_c * width_q
    more = () if add is None else (add,)
    add_spec = pl.BlockSpec((tile_a, width_b, pairs), lambda i, w: (i, 0, 0))
    if last:
        shape = (width_a // tile_a, pairs, tile_a * width_b)
        out_spec = pl.BlockSpec((None, *shape[1:]), lambda i, w: (i, 0, 0))
    else:
        shape, out_spec = (width_a, width_b, pairs), add_spec
    return pl.pallas_call(
        functools.partial(ladder_kernel, plans, len(operands), add is None, last, parts),
        grid_spec=pltpu.PrefetchScalarGridSpec(
            num_scalar_prefetch=1,
            grid=(width_a // tile_a,),
            in_specs=[pl.BlockSpec(memory_space=pl.ANY)] * len(operands) + [add_spec] * len(more),
            out_specs=out_spec,
            scratch_shapes=scratch,
        ),
        out_shape=jax.ShapeDtypeStruct(shape, jnp.float32),
        input_output_aliases={len(operands) + 1: 0} if more and not last else {},
        cost_estimate=pl.CostEstimate(flops=2 * products, bytes_accessed=moved, transcendentals=0),
        compiler_params=pltpu.CompilerParams(vmem_limit_bytes=vmem * 2**20),
        name="ladder",
    )(which, *operands, *more)


def by_lines(n_row, n_col, *arrays):
    left_factors, right_factors, amplitudes, eps_left, eps_right, pair_energy = arrays
    row, col = lax.axis_index("row"), lax.axis_index("col")
    n_z, n_y = n_row // 2, n_col // 2
    z, x, y, core = row // 2, row % 2, col // 2, col % 2
    half = n_z // 2

    def inner(at):
        return at in (half - 1, half)

    before = []

    def send(value, place):
        pairs = []
        for at_z in range(n_z):
            for at_x in range(2):
                for at_y in range(n_y):
                    for at_k in range(2):
                        to = place(at_z, at_x, at_y, at_k)
                        if to is not None:
                            source = (at_z * 2 + at_x) * n_col + at_y * 2 + at_k
                            target = (to[0] * 2 + to[1]) * n_col + to[2] * 2 + to[3]
                            pairs.append((source, target))
        return lax.ppermute(value, AXES, pairs)

    def now(*values):
        return lax.optimization_barrier((values, tuple(before)))[0]

    def step(*transfers, beside=()):
        values = now(*(value for value, _ in transfers))
        got = [send(value, place) for value, (_, place) in zip(values, transfers)]
        before[:] = [*got, *beside]
        return got

    def other_x(c, x, y, k):
        return c, 1 - x, y, k

    def other_y(c, x, y, k):
        return c, x, 1 - y, k

    def other_core(c, x, y, k):
        return c, x, y, 1 - k

    def near(c, x, y, k):
        return c ^ 1, x, y, k

    def across(c, x, y, k):
        return (n_z - 1 - c, x, y, k) if inner(c) else None

    def outward(c, x, y, k):
        return (c ^ 1, x, y, k) if inner(c) else None

    def between_inner(step):
        return lambda c, x, y, k: step(c, x, y, k) if inner(c) else None

    is_inner = (z == half - 1) | (z == half)
    at_far = y == 1 - z // half

    width_a, local_c, local_q = left_factors.shape
    mine = left_factors.reshape(width_a, local_c, 2, local_q // 2).transpose(2, 0, 1, 3)

    local_d = right_factors.shape[0]
    width_b = eps_right.shape[0]
    part_d = local_d // 4
    depth = part_d // 2

    def right_part(at_x, part, right=right_factors):
        rows = lax.dynamic_slice_in_dim(right, at_x * 2 * part_d + part * part_d, part_d)
        return rows.reshape(part_d, -1, width_b).transpose(0, 2, 1)

    def amp_part(at_x, part, amp):
        got = lax.dynamic_slice_in_dim(amp, at_x * 2 * part_d + part * part_d, part_d, 1)
        return got.transpose(1, 0, 2)

    def both(one, two, at):
        rows = slice(at * depth, (at + 1) * depth)
        return jnp.stack([one[rows], two[rows]])

    def either(inner_one, end_one):
        return jnp.where(is_inner, inner_one, end_one.reshape(inner_one.shape)), near

    far_inner = jnp.where(z < half, half, half - 1)
    planes = (z, z ^ 1, far_inner, far_inner ^ 1)
    which = jnp.stack([v for p in planes for v in (p ^ col, x, p ^ col, 1 - x)] + [jnp.zeros_like(x)])
    turn = jnp.where(is_inner & at_far, 1, 0)
    choice = jnp.where(is_inner, 0, jnp.where(at_far, 1, 2))
    which_far = [v for p in planes[2:] for v in ((p % 2) ^ core, x ^ turn, (p % 2) ^ core, 1 - x ^ turn)]
    which_far = jnp.stack(which_far + [choice])

    mine, x_give, o_full = lax.optimization_barrier((mine, right_part(1 - x, 0), right_part(x, 0)))
    before[:] = [x_give, o_full]
    (right_later,) = now(right_factors)
    near_o, far_o, x_full, y_0 = step(
        (o_full, near), (o_full, across), (x_give, other_x), (mine[0], other_y)
    )
    give_split, o_split = right_part(1 - x, 1, right_later), right_part(x, 1, right_later)
    before += [give_split, o_split]

    (amp_later,) = now(amplitudes)
    out_o, far_x, x_0, y_1, mine_k = step(
        either(far_o, jnp.where(at_far, mine[1], y_0)),
        (x_full, across),
        (mine[0], other_x),
        (mine[1], other_y),
        (mine, other_core),
    )
    amp_full, amp_give = amp_part(x, 0, amp_later), amp_part(1 - x, 0, amp_later)
    amp_own, amp_late = amp_part(x, 1, amp_later), amp_part(1 - x, 1, amp_later)
    mixed = [both(give_split, amp_give, i) for i in range(2)]
    before += [amp_full, amp_own, amp_late, *mixed]

    near_x, third_o, x_1, xy_0, first_k = step(
        (x_full, near),
        (near_o, across),
        (mine[1], other_x),
        (x_0, other_y),
        (jnp.stack([y_0, y_1, x_0]), other_core),
    )
    out_x, third_x, mixed[0], xy_1, second_k = step(
        either(far_x, jnp.where(at_far, x_1, xy_0)),
        (near_x, across),
        (mixed[0], other_x),
        (x_1, other_y),
        (jnp.stack([x_1, xy_0]), other_core),
    )
    split = [jnp.stack([o_split[:depth], mixed[0][0]])]
    beside, far_split, third_split = [None, None], [None, None], [None, None]
    beside[0], far_split[0], mixed[1], end_y, xy_k = step(
        (split[0], near),
        (split[0], across),
        (mixed[1], other_x),
        (out_o, between_inner(other_y)),
        (xy_1, other_core),
    )
    mine_0, mine_1 = mine[0], mine[1]
    lefts = [(mine_0, None), (mine_1, None), (x_0, None), (x_1, None)]
    lefts += [(mine_k, 0), (mine_k, 1), (first_k, 2), (second_k, 0)]
    lefts += [(y_0, None), (y_1, None), (xy_0, None), (xy_1, None)]
    lefts += [(first_k, 0), (first_k, 1), (second_k, 1), (xy_k, None)]

    def full(i):
        pieces = [(v, i) for v in (o_full, x_full, near_o, near_x, far_o, far_x, third_o, third_x)]
        return [(pieces, lefts, [(amp_full, i), (mixed[i], 1)])]

    def parted(i):
        pieces = [(v, h) for v in (split[i], beside[i], far_split[i], third_split[i]) for h in range(2)]
        return [(pieces, lefts, [(amp_own, i), (amp_late, i)])]

    def far_half(from_near):
        ends = [(out_o, None), (end_y, None), (out_x, None), (end_xy, None)]
        ends += [(end_k, 0), (end_yk, 0), (end_k, 1), (end_yk, 1)]
        got = [(v, h) for h in range(2) for v in from_near]
        pieces = [(v, h) for vs in (far_split, third_split) for h in range(2) for v in vs]
        own = [(v, i) for v in (out_o, out_x) for i in range(2)] + got
        amps = [(amp_full, 0), (amp_full, 1), (mixed[0], 1), (mixed[1], 1)]
        return [(pieces, ends, got), *((own, v, amps) for v in (lefts[:8], lefts[8:]))]

    total = add_ladder([full(0)], which, None, depth)
    before.append(total)
    mixed[1], third_o, third_x = now(mixed[1], third_o, third_x)
    split.append(jnp.stack([o_split[depth:], mixed[1][0]]))
    beside[1], third_split[0], amp_late, end_xy, far_split[1] = step(
        (split[1], near),
        (beside[0], across),
        (amp_late, other_x),
        (out_x, between_inner(other_y)),
        (split[1], across),
    )
    del before[-1]
    total = add_ladder([full(1)], which, total, depth)
    before.append(total)
    amp_own, amp_late, third_o, third_x, end_y, end_xy = now(
        amp_own, amp_late, third_o, third_x, end_y, end_xy
    )
    e7, third_split[1], end_yk, end_k = step(
        either(both(third_o, third_x, 0), both(amp_own, amp_late, 0)),
        (beside[1], across),
        (jnp.stack([end_y, end_xy]), other_core),
        (jnp.stack([out_o, out_x]), other_core),
    )
    del before[1]
    total = add_ladder([parted(0)], which, total, depth)
    before.append(total)
    third_o, third_x, amp_own, amp_late = now(third_o, third_x, amp_own, amp_late)
    (e8,) = step(either(both(third_o, third_x, 1), both(amp_own, amp_late, 1)))
    total = add_ladder([parted(1)], which, total, depth)
    total = add_ladder([far_half((e7, e8))], which_far, total, depth, True, parts=2)

    def pick(value, at):
        return lax.dynamic_index_in_dim(value, at, 0, keepdims=False)

    pairs = amplitudes.shape[2]
    own_a, own_pairs = width_a // n_col, pairs // n_row
    total = total.reshape(n_y, 2, pairs, own_a * width_b)
    keep = lax.dynamic_index_in_dim(total, core, 1, keepdims=False)
    give = lax.dynamic_index_in_dim(total, 1 - core, 1, keepdims=False)
    part = keep + send(give, other_core)
    part = part.reshape(n_y, n_z, 2, own_pairs, own_a * width_b)

    def over_x(v):
        own, other = (lax.dynamic_index_in_dim(v, at, -3, keepdims=False) for at in (x, 1 - x))
        return own + send(other, other_x)

    def over_y(v):
        return pick(v, y) + send(pick(v, 1 - y), other_y)

    cut = own_pairs // 2
    first = over_y(over_x(part[..., :cut, :]))
    second = over_x(over_y(part[..., cut:, :]))
    part = jnp.concatenate([first, second], axis=1)
    ladder = pick(part, z)
    for step in range(1, n_z):
        ladder = ladder + send(pick(part, z ^ step), lambda c, x, y, k, s=step: (c ^ s, x, y, k))
    ladder = ladder.reshape(own_pairs, own_a, width_b)
    denom = eps_left[None, :, None] + eps_right[None, None, :] - pair_energy[:, None, None]
    return ladder / denom


def solution(mesh):
    n_row, n_col = mesh.shape["row"], mesh.shape["col"]
    lines = n_row == 2 * n_col and n_col == 4
    per_device = functools.partial(by_lines, n_row, n_col) if lines else gathered_whole
    in_specs = (
        P(None, "row", "col"),
        P("col", "row"),
        P("row", "col", None),
        P("col"),
        P(),
        P("row"),
    )
    out_specs = P("row", "col", None)
    return jax.shard_map(
        per_device, mesh=mesh, in_specs=in_specs, out_specs=out_specs, check_vma=False
    )
```

```python
import functools

import jax
import jax.numpy as jnp
from jax import lax
from jax.experimental import pallas as pl
from jax.experimental.pallas import tpu as pltpu
from jax.sharding import PartitionSpec as P

AXES = ("row", "col")
PART_A = 4


def contract_aux(left_piece, right_piece):
    return lax.dot_general(
        left_piece, right_piece, (((2,), (1,)), ((), ())), preferred_element_type=jnp.float32
    )


def gathered_whole(left_factors, right_factors, amplitudes, eps_left, eps_right, pair_energy):
    width_a, local_c, _ = left_factors.shape
    local_d = right_factors.shape[0]
    width_b = eps_right.shape[0]
    pairs = amplitudes.shape[2]
    gathered = lax.all_gather(right_factors, "row", axis=1, tiled=True)
    right_whole = gathered.reshape(local_d, -1, width_b)
    left_whole = lax.all_gather(left_factors, "col", axis=2, tiled=True)
    integ = contract_aux(left_whole, right_whole)
    integ = integ.astype(jnp.bfloat16)
    n_row = lax.axis_size("row")
    n_col = lax.axis_size("col")
    own_pairs = pairs // n_row
    own_a = width_a // n_col
    partial_value = jnp.einsum(
        "cdp,acdb->pab", amplitudes, integ, preferred_element_type=jnp.float32
    )
    partial_value = partial_value.reshape(pairs, width_a * width_b)
    section = lax.psum_scatter(partial_value, "row", scatter_dimension=0, tiled=True)
    ladder = lax.psum_scatter(section, "col", scatter_dimension=1, tiled=True)
    ladder = ladder.reshape(own_pairs, own_a, width_b)
    denom = eps_left[None, :, None] + eps_right[None, None, :] - pair_energy[:, None, None]
    return ladder / denom


def ladder_kernel(plans, operands, first, last, parts, which_ref, *refs):
    inputs, refs = refs[:operands], refs[operands:]
    *add_ref, out_ref = refs[: 1 if first else 2]
    scratch = refs[1 if first else 2 :]
    held_shape = scratch[2].shape
    tile_a, chunk_c, width_q = held_shape[3], held_shape[5], held_shape[6]
    _, depth, width_b, _ = scratch[0].shape
    span, sub = 2 * chunk_c, depth // parts
    step, steps = pl.program_id(0), pl.num_programs(0)
    slot = lax.rem(step, 2)

    def view(entry, rows):
        operand, place = entry
        ref = inputs[operand]
        if rows is None:
            return ref.at[place] if len(ref.shape) == 4 else ref.at[pl.ds(place * sub, sub)]
        return ref.at[rows] if place is None else ref.at[place, rows]

    def whole(group, choice):
        pieces, _, amps = plans[group][choice]
        right, amp, _, sems, _ = scratch[5 * group : 5 * group + 5]
        at = [(n // parts, pl.ds(n % parts * sub, sub)) for n in range(len(pieces))]
        pairs = [(v, right.at[s, rows]) for v, (s, rows) in zip(pieces, at)]
        pairs += [(v, amp.at[rows, s]) for v, (s, rows) in zip(amps, at)]
        return [
            pltpu.make_async_copy(view(v, None), to, sems.at[n]) for n, (v, to) in enumerate(pairs)
        ]

    def tiles(group, choice, at, slot):
        lefts = plans[group][choice][1]
        held, sems = scratch[5 * group + 2], scratch[5 * group + 4]
        rows = pl.ds(pl.multiple_of(at * tile_a, tile_a), tile_a)
        return [
            pltpu.make_async_copy(
                view(lefts[4 * r + 2 * s + h], rows), held.at[slot, r, h, :, s], sems.at[slot, r, h, s]
            )
            for r in range(len(lefts) // 4)
            for h in range(2)
            for s in range(2)
        ]

    ends = []
    for plan in plans:
        ends.append((ends[-1] if ends else 0) + 2 * len(plan[0][0]) // parts + 1)

    def start(group, copies):
        plan = plans[group]
        for choice in range(len(plan)):

            def go():
                for copy in copies(choice):
                    copy.start()

            if len(plan) == 1:
                go()
            else:
                pl.when(which_ref[ends[group] - 1] == choice)(go)

    @pl.when(step == 0)
    def _():
        for group in range(len(plans)):
            start(group, lambda choice: whole(group, choice) + tiles(group, choice, step, 0))

    @pl.when(step + 1 < steps)
    def _():
        for group in range(len(plans)):
            start(group, lambda choice: tiles(group, choice, step + 1, 1 - slot))

    def product(group, rows):
        slots = len(plans[group][0][0]) // parts
        right, amp, held = scratch[5 * group : 5 * group + 3]
        base = ends[group] - 2 * slots - 1
        integ = None
        for s in range(slots):
            left = held[slot, which_ref[base + 2 * s], which_ref[base + 2 * s + 1], rows]
            term = lax.dot_general(
                right[s].reshape(depth * width_b, width_q),
                left.reshape(-1, width_q),
                (((1,), (1,)), ((), ())),
                preferred_element_type=jnp.float32,
            )
            integ = term if integ is None else integ + term
        integ = integ.astype(jnp.bfloat16)
        integ = jnp.concatenate(
            [
                jnp.concatenate(
                    [
                        integ[d * width_b : (d + 1) * width_b, a * span : (a + 1) * span]
                        for d in range(depth)
                    ],
                    axis=1,
                )
                for a in range(integ.shape[1] // span)
            ],
            axis=0,
        )
        both = amp[...].reshape(depth * span, -1)
        return jnp.dot(integ, both, preferred_element_type=jnp.float32)

    for group in range(len(plans)):

        @pl.when(step == 0)
        def _():
            for copy in whole(group, 0):
                copy.wait()

        for copy in tiles(group, 0, step, slot):
            copy.wait()
        for at in range(0, tile_a, PART_A):
            rows = slice(at, at + PART_A)
            out = product(group, rows).reshape(PART_A, width_b, -1)
            out = out if first else add_ref[0][rows] + out
            if last:
                out_ref[:, at * width_b : (at + PART_A) * width_b] = out.reshape(-1, out.shape[-1]).T
            else:
                out_ref[rows] = out


def add_ladder(groups, which, add, depth, last=False, vmem=44, parts=1):
    operands, plans = [], []
    depth *= parts
    for group in groups:
        plan = []
        for choice in group:
            entries = []
            for part in choice:
                for array, _ in part:
                    if not any(array is v for v in operands):
                        operands.append(array)
                entries.append(
                    [(next(n for n, v in enumerate(operands) if v is a), place) for a, place in part]
                )
            plan.append(entries)
        plans.append(plan)
    pieces, lefts, amps = groups[0][0]
    width_b, width_q = pieces[0][0].shape[-2:]
    width_a, chunk_c = lefts[0][0].shape[-3:-1]
    pairs = amps[0][0].shape[-1]
    tile_a = 2 * PART_A
    scratch, products, moved = [], 0, 8 * width_a * width_b * pairs
    for group in groups:
        slots, n_left = len(group[0][0]) // parts, len(group[0][1]) // 4
        scratch += [
            pltpu.VMEM((slots, depth, width_b, width_q), jnp.bfloat16),
            pltpu.VMEM((depth, 2, chunk_c, pairs), jnp.bfloat16),
            pltpu.VMEM((2, n_left, 2, tile_a, 2, chunk_c, width_q), jnp.bfloat16),
            pltpu.SemaphoreType.DMA(((slots + 2) * parts,)),
            pltpu.SemaphoreType.DMA((2, n_left, 2, 2)),
        ]
        products += depth * width_b * width_a * 2 * chunk_c * (slots * width_q + pairs)
        moved += 2 * depth * (slots * width_b * width_q + 2 * chunk_c * pairs)
        moved += 8 * n_left * width_a * chunk_c * width_q
    more = () if add is None else (add,)
    add_spec = pl.BlockSpec((tile_a, width_b, pairs), lambda i, w: (i, 0, 0))
    if last:
        shape = (width_a // tile_a, pairs, tile_a * width_b)
        out_spec = pl.BlockSpec((None, *shape[1:]), lambda i, w: (i, 0, 0))
    else:
        shape, out_spec = (width_a, width_b, pairs), add_spec
    return pl.pallas_call(
        functools.partial(ladder_kernel, plans, len(operands), add is None, last, parts),
        grid_spec=pltpu.PrefetchScalarGridSpec(
            num_scalar_prefetch=1,
            grid=(width_a // tile_a,),
            in_specs=[pl.BlockSpec(memory_space=pl.ANY)] * len(operands) + [add_spec] * len(more),
            out_specs=out_spec,
            scratch_shapes=scratch,
        ),
        out_shape=jax.ShapeDtypeStruct(shape, jnp.float32),
        input_output_aliases={len(operands) + 1: 0} if more and not last else {},
        cost_estimate=pl.CostEstimate(flops=2 * products, bytes_accessed=moved, transcendentals=0),
        compiler_params=pltpu.CompilerParams(vmem_limit_bytes=vmem * 2**20),
        name="ladder",
    )(which, *operands, *more)


def by_lines(n_row, n_col, *arrays):
    left_factors, right_factors, amplitudes, eps_left, eps_right, pair_energy = arrays
    row, col = lax.axis_index("row"), lax.axis_index("col")
    n_z, n_y = n_row // 2, n_col // 2
    z, x, y, core = row // 2, row % 2, col // 2, col % 2
    half = n_z // 2

    def inner(at):
        return at in (half - 1, half)

    before = []

    def send(value, place):
        pairs = []
        for at_z in range(n_z):
            for at_x in range(2):
                for at_y in range(n_y):
                    for at_k in range(2):
                        to = place(at_z, at_x, at_y, at_k)
                        if to is not None:
                            source = (at_z * 2 + at_x) * n_col + at_y * 2 + at_k
                            target = (to[0] * 2 + to[1]) * n_col + to[2] * 2 + to[3]
                            pairs.append((source, target))
        return lax.ppermute(value, AXES, pairs)

    def now(*values):
        return lax.optimization_barrier((values, tuple(before)))[0]

    def step(*transfers, beside=()):
        values = now(*(value for value, _ in transfers))
        got = [send(value, place) for value, (_, place) in zip(values, transfers)]
        before[:] = [*got, *beside]
        return got

    def other_x(c, x, y, k):
        return c, 1 - x, y, k

    def other_y(c, x, y, k):
        return c, x, 1 - y, k

    def other_core(c, x, y, k):
        return c, x, y, 1 - k

    def near(c, x, y, k):
        return c ^ 1, x, y, k

    def across(c, x, y, k):
        return (n_z - 1 - c, x, y, k) if inner(c) else None

    def outward(c, x, y, k):
        return (c ^ 1, x, y, k) if inner(c) else None

    def between_inner(step):
        return lambda c, x, y, k: step(c, x, y, k) if inner(c) else None

    is_inner = (z == half - 1) | (z == half)
    at_far = y == 1 - z // half

    width_a, local_c, local_q = left_factors.shape
    mine = left_factors.reshape(width_a, local_c, 2, local_q // 2).transpose(2, 0, 1, 3)

    local_d = right_factors.shape[0]
    width_b = eps_right.shape[0]
    part_d = local_d // 4
    depth = part_d // 2

    def right_part(at_x, part, right=right_factors):
        rows = lax.dynamic_slice_in_dim(right, at_x * 2 * part_d + part * part_d, part_d)
        return rows.reshape(part_d, -1, width_b).transpose(0, 2, 1)

    def amp_part(at_x, part, amp):
        got = lax.dynamic_slice_in_dim(amp, at_x * 2 * part_d + part * part_d, part_d, 1)
        return got.transpose(1, 0, 2)

    def both(one, two, at):
        rows = slice(at * depth, (at + 1) * depth)
        return jnp.stack([one[rows], two[rows]])

    def either(inner_one, end_one):
        return jnp.where(is_inner, inner_one, end_one.reshape(inner_one.shape)), near

    far_inner = jnp.where(z < half, half, half - 1)
    planes = (z, z ^ 1, far_inner, far_inner ^ 1)
    which = jnp.stack([v for p in planes for v in (p ^ col, x, p ^ col, 1 - x)] + [jnp.zeros_like(x)])
    turn = jnp.where(is_inner & at_far, 1, 0)
    choice = jnp.where(is_inner, 0, jnp.where(at_far, 1, 2))
    which_far = [v for p in planes[2:] for v in ((p % 2) ^ core, x ^ turn, (p % 2) ^ core, 1 - x ^ turn)]
    which_far = jnp.stack(which_far + [choice])

    mine, x_give, o_full = lax.optimization_barrier((mine, right_part(1 - x, 0), right_part(x, 0)))
    before[:] = [x_give, o_full]
    (right_later,) = now(right_factors)
    near_o, far_o, x_full, y_0 = step(
        (o_full, near), (o_full, across), (x_give, other_x), (mine[0], other_y)
    )
    give_split, o_split = right_part(1 - x, 1, right_later), right_part(x, 1, right_later)
    before += [give_split, o_split]

    (amp_later,) = now(amplitudes)
    out_o, far_x, x_0, y_1, mine_k = step(
        either(far_o, jnp.where(at_far, mine[1], y_0)),
        (x_full, across),
        (mine[0], other_x),
        (mine[1], other_y),
        (mine, other_core),
    )
    amp_full, amp_give = amp_part(x, 0, amp_later), amp_part(1 - x, 0, amp_later)
    amp_own, amp_late = amp_part(x, 1, amp_later), amp_part(1 - x, 1, amp_later)
    mixed = [both(give_split, amp_give, i) for i in range(2)]
    before += [amp_full, amp_own, amp_late, *mixed]

    near_x, third_o, x_1, xy_0, first_k = step(
        (x_full, near),
        (near_o, across),
        (mine[1], other_x),
        (x_0, other_y),
        (jnp.stack([y_0, y_1, x_0]), other_core),
    )
    out_x, third_x, mixed[0], xy_1, second_k = step(
        either(far_x, jnp.where(at_far, x_1, xy_0)),
        (near_x, across),
        (mixed[0], other_x),
        (x_1, other_y),
        (jnp.stack([x_1, xy_0]), other_core),
    )
    split = [jnp.stack([o_split[:depth], mixed[0][0]])]
    beside, far_split, third_split = [None, None], [None, None], [None, None]
    beside[0], far_split[0], mixed[1], end_y, xy_k = step(
        (split[0], near),
        (split[0], across),
        (mixed[1], other_x),
        (out_o, between_inner(other_y)),
        (xy_1, other_core),
    )
    mine_0, mine_1 = mine[0], mine[1]
    lefts = [(mine_0, None), (mine_1, None), (x_0, None), (x_1, None)]
    lefts += [(mine_k, 0), (mine_k, 1), (first_k, 2), (second_k, 0)]
    lefts += [(y_0, None), (y_1, None), (xy_0, None), (xy_1, None)]
    lefts += [(first_k, 0), (first_k, 1), (second_k, 1), (xy_k, None)]

    def full(i):
        pieces = [(v, i) for v in (o_full, x_full, near_o, near_x, far_o, far_x, third_o, third_x)]
        return [(pieces, lefts, [(amp_full, i), (mixed[i], 1)])]

    def parted(i):
        pieces = [(v, h) for v in (split[i], beside[i], far_split[i], third_split[i]) for h in range(2)]
        return [(pieces, lefts, [(amp_own, i), (amp_late, i)])]

    def far_half(from_near):
        ends = [(out_o, None), (end_y, None), (out_x, None), (end_xy, None)]
        ends += [(end_k, 0), (end_yk, 0), (end_k, 1), (end_yk, 1)]
        got = [(v, h) for h in range(2) for v in from_near]
        pieces = [(v, h) for vs in (far_split, third_split) for h in range(2) for v in vs]
        own = [(v, i) for v in (out_o, out_x) for i in range(2)] + got
        amps = [(amp_full, 0), (amp_full, 1), (mixed[0], 1), (mixed[1], 1)]
        return [(pieces, ends, got), *((own, v, amps) for v in (lefts[:8], lefts[8:]))]

    total = add_ladder([full(0)], which, None, depth)
    before.append(total)
    mixed[1], third_o, third_x = now(mixed[1], third_o, third_x)
    split.append(jnp.stack([o_split[depth:], mixed[1][0]]))
    beside[1], third_split[0], amp_late, end_xy, far_split[1] = step(
        (split[1], near),
        (beside[0], across),
        (amp_late, other_x),
        (out_x, between_inner(other_y)),
        (split[1], across),
    )
    del before[-1]
    total = add_ladder([full(1)], which, total, depth)
    before.append(total)
    amp_own, amp_late, third_o, third_x, end_y, end_xy = now(
        amp_own, amp_late, third_o, third_x, end_y, end_xy
    )
    e7, third_split[1], end_yk, end_k = step(
        either(both(third_o, third_x, 0), both(amp_own, amp_late, 0)),
        (beside[1], across),
        (jnp.stack([end_y, end_xy]), other_core),
        (jnp.stack([out_o, out_x]), other_core),
    )
    del before[1]
    total = add_ladder([parted(0)], which, total, depth)
    before.append(total)
    third_o, third_x, amp_own, amp_late = now(third_o, third_x, amp_own, amp_late)
    (e8,) = step(either(both(third_o, third_x, 1), both(amp_own, amp_late, 1)))
    total = add_ladder([parted(1)], which, total, depth)
    total = add_ladder([far_half((e7, e8))], which_far, total, depth, True, 58, 2)

    def pick(value, at):
        return lax.dynamic_index_in_dim(value, at, 0, keepdims=False)

    pairs = amplitudes.shape[2]
    own_a, own_pairs = width_a // n_col, pairs // n_row
    total = total.reshape(n_y, 2, pairs, own_a * width_b)
    keep = lax.dynamic_index_in_dim(total, core, 1, keepdims=False)
    give = lax.dynamic_index_in_dim(total, 1 - core, 1, keepdims=False)
    part = keep + send(give, other_core)
    part = part.reshape(n_y, n_z, 2, own_pairs, own_a * width_b)

    def over_x(v):
        own, other = (lax.dynamic_index_in_dim(v, at, -3, keepdims=False) for at in (x, 1 - x))
        return own + send(other, other_x)

    def over_y(v):
        return pick(v, y) + send(pick(v, 1 - y), other_y)

    cut = own_pairs // 2
    first = over_y(over_x(part[..., :cut, :]))
    second = over_x(over_y(part[..., cut:, :]))
    part = jnp.concatenate([first, second], axis=1)
    ladder = pick(part, z)
    for step in range(1, n_z):
        ladder = ladder + send(pick(part, z ^ step), lambda c, x, y, k, s=step: (c ^ s, x, y, k))
    ladder = ladder.reshape(own_pairs, own_a, width_b)
    denom = eps_left[None, :, None] + eps_right[None, None, :] - pair_energy[:, None, None]
    return ladder / denom


def solution(mesh):
    n_row, n_col = mesh.shape["row"], mesh.shape["col"]
    lines = n_row == 2 * n_col and n_col == 4
    per_device = functools.partial(by_lines, n_row, n_col) if lines else gathered_whole
    in_specs = (
        P(None, "row", "col"),
        P("col", "row"),
        P("row", "col", None),
        P("col"),
        P(),
        P("row"),
    )
    out_specs = P("row", "col", None)
    return jax.shard_map(
        per_device, mesh=mesh, in_specs=in_specs, out_specs=out_specs, check_vma=False
    )
```
